32 devices in a mesh: art: 16 (over z, y, core), seq: 2 (over x).
Axes of the slice: x: 2, y: 2, z: 4, core: 2. Of those that a mesh axis runs over, the one named last changes fastest.
Arguments:
- queries: bfloat16 [192, 2, 256, 128], P('art', 'seq'), may hold values from -6 to 6
- cand_owner: int32 [384, 16, 4], P(('art', 'seq')), may hold values from 0 to 15, all different within a row; in each aligned block of 192 rows (0 to 191, 192 to 383, ..., all dimensions but the last counted through in order) at most 72 rows name the same one
- cand_local: int32 [384, 16, 4], P(('art', 'seq')), may hold values from 0 to 255, as said below
- companies: bfloat16 [4096, 64, 128], P('art'), may hold values from -6 to 6
Outputs:
- relevance: float32 [384, 64], P(('art', 'seq'))
- probs: float32 [384, 64], P(('art', 'seq'))
The draws below stay inside these ranges and needn't reach their ends.
Inputs may be any that keep to these rules, and one draw needn't show every extreme that they name: `cand_owner`: each row of four candidates names four different owners. Among the candidates of one device's 12 articles (aligned blocks of 12 articles in the order of the array), no owner is named more than 72 times, a bound that some block reaches. `cand_local`: the candidates of one device's 12 articles (aligned blocks of 12 articles in the order of the array) name exactly 36 different local indices in all.
All inputs are finite; a program needn't handle non-finite values.
Results may differ from the reference program's by a relative error of at most 0.0088.
Values may be sent and summed in bfloat16 or wider, within the bound.
No kernel may reach another device: no remote copies, remote signals or barrier semaphores. Data moves between devices by JAX's collectives and lax.ppermute only.
A program may use at most 128 MiB of HBM per device.

```python
import math
import jax
import jax.numpy as jnp
import numpy as np
from jax import lax

E = 128
LQ = 256
LC = 64
NC = 64
A_DEV = 12
C_DEV = 256
CAP = 72
DIST = 36
ARTICLES = 384
COMPANIES = 4096
N_ART = 16
N_SEQ = 2


def draw_cand_local(key, part):
    block_count = ARTICLES // A_DEV
    per_block = A_DEV * NC
    stride = C_DEV // DIST
    keys = jax.random.split(key, block_count + 1)
    spread = jax.random.randint(keys[0], (block_count,), 0, C_DEV)
    base = spread * spread // C_DEV
    base = base.at[0].set(C_DEV - 1).at[1].set(0)
    order = jax.vmap(lambda k: jax.random.permutation(k, per_block))(keys[1:]) % DIST
    local = (base[:, None] + order * stride) % C_DEV
    return local.reshape(ARTICLES, NC // 4, 4).astype(jnp.int32)


def shard_levels(own_key, extent, cuts, low, top_value):
    def one(dim, shards_of):
        steps = jax.random.uniform(jax.random.fold_in(jax.random.fold_in(own_key, 6), dim), (shards_of,), jnp.float32, low / len(cuts), top_value / len(cuts))
        return jnp.repeat(jnp.exp(steps), extent[dim] // shards_of).reshape((-1,) + (1,) * (len(extent) - dim - 1))

    level = one(*cuts[0])
    for cut in cuts[1:]:
        level = level * one(*cut)
    return level


def assign_block(own_key, own, number, rows, number_of, top, bound, skew):
    sequence = jax.random.permutation(own_key, number_of)
    crowded, ordinary = portions_of(number_of, rows * top, bound, skew, True), portions_of(number_of, rows * top, bound, skew, False)
    places = jnp.arange(number_of)

    def named(tallies, rotation):
        used = int((tallies > 0).sum())
        fixed = max(1, used // 4)
        passed = fixed + (places - fixed + rotation * (used - fixed)) % max(1, number_of - fixed)
        return jnp.zeros((number_of,), jnp.int32).at[sequence[jnp.where(places < fixed, places, passed)]].set(jnp.asarray(tallies, jnp.int32))

    tallies = jnp.where(number % 4 == 0, named(crowded, number // 4), named(ordinary, number - number // 4 - 1))
    mixed = jax.random.permutation(jax.random.fold_in(own, 3), number_of)
    giver, taker = mixed[0:number_of // 2 * 2:2], mixed[1:number_of // 2 * 2:2]
    margin = jnp.minimum(tallies[giver] - 1, bound - tallies[taker]) // 2
    margin = jnp.where((giver == sequence[0]) | (taker == sequence[0]) | (tallies[taker] == 0), 0, jnp.maximum(margin, 0))
    passed = jax.random.randint(jax.random.fold_in(own, 4), (number_of // 2,), 0, 1 << 20) % (margin + 1)
    tallies = tallies.at[giver].add(-passed).at[taker].add(passed)
    items = jnp.searchsorted(jnp.cumsum(tallies), jnp.arange(rows * top), side="right").astype(jnp.int32)
    grid = items.reshape(top, rows).T
    grid = grid[jax.random.permutation(jax.random.fold_in(own, 1), rows)]
    rotation = jax.random.randint(jax.random.fold_in(own, 2), (rows, 1), 0, top)
    return jnp.take_along_axis(grid, (jnp.arange(top)[None, :] + rotation) % top, axis=1)


def portions_of(amount, total, most, lean, full):
    loads = [(1 << 20) // math.isqrt(grade ** lean) + 1 for grade in range(1, amount + 1)]
    largest = most if full else min(most, max(-(-total // amount), total * loads[0] // sum(loads)))
    least = 1 if total - largest >= amount - 1 else 0
    given, rest = [largest] + [least] * (amount - 1), total - largest - least * (amount - 1)
    while rest > 0:
        free = [i for i in range(1, amount) if given[i] < largest] or [i for i in range(1, amount) if given[i] < most]
        pool, remaining = sum([loads[i] for i in free]), rest
        for i in free:
            extra = min(most - given[i], max(1, remaining * loads[i] // pool), rest)
            given[i] = given[i] + extra
            rest = rest - extra
    return np.array(given)


def scatter_about(key, extent, deviation, reach, cuts=(), held_as=jnp.bfloat16):
    loudness = shard_levels(key, extent, cuts, -0.22, 0.18) if cuts else 1.0
    array = jax.random.normal(key, extent, jnp.float32) * deviation * loudness
    return jnp.minimum(jnp.maximum(array, -reach), reach).astype(held_as)


def setup_inputs(seed: int = 0) -> dict:
    streams_of = jax.random.split(jax.random.key(seed), 5)
    queries = scatter_about(streams_of[0], (ARTICLES // N_SEQ, N_SEQ, LQ, E), 1.0, 6.0, ((0, 16), (1, 2)))
    cand_owner_keys = jax.random.split(jax.random.fold_in(streams_of[1], 1), ARTICLES * (NC // 4) // (A_DEV * NC // 4))
    cand_owner_turns = jax.random.permutation(jax.random.fold_in(streams_of[1], 3), ARTICLES * (NC // 4) // (A_DEV * NC // 4))
    cand_owner = jax.vmap(lambda own, number: assign_block(jax.random.fold_in(streams_of[1], 2), own, number, A_DEV * NC // 4, N_ART, 4, CAP, 2))(cand_owner_keys, cand_owner_turns).reshape((ARTICLES, NC // 4, 4))
    cand_local = draw_cand_local(jax.random.fold_in(streams_of[4], 71), 0)
    companies = scatter_about(streams_of[3], (COMPANIES, LC, E), 1.0, 6.0, ((0, 16),))
    return dict(queries=queries, cand_owner=cand_owner, cand_local=cand_local, companies=companies)


EPS = 1e-06
SHARP = 16.0
TEMPER = 4.0

def unit_rows(values):
    wide = values.astype(jnp.float32)
    return (wide * lax.rsqrt(lax.optimization_barrier(jnp.sum(wide * wide, axis=-1, keepdims=True)) + EPS)).astype(jnp.bfloat16)

def reference(queries, cand_owner, cand_local, companies):
    query_unit = unit_rows(queries.reshape(ARTICLES, LQ, E))
    company_unit = unit_rows(companies)
    cand_id = (cand_owner * C_DEV + cand_local).reshape(ARTICLES, NC).astype(jnp.int32)

    def one_article(pair):
        query_rows, ids = pair
        blocks = company_unit[ids].reshape(NC * LC, E)
        sims = jnp.dot(query_rows.astype(jnp.float32), blocks.astype(jnp.float32).T, preferred_element_type=jnp.float32)
        mass = lax.optimization_barrier(jnp.sum(jnp.exp(sims * SHARP).reshape(LQ, NC, LC), axis=-1))
        return lax.optimization_barrier(jnp.sum(jnp.log(mass), axis=0)) / SHARP
    score = lax.map(one_article, (query_unit, cand_id))
    relevance = score - lax.optimization_barrier(jnp.mean(score, axis=-1, keepdims=True))
    weights = jnp.exp(TEMPER * relevance)
    probs = weights / lax.optimization_barrier(jnp.sum(weights, axis=-1, keepdims=True))
    return (relevance, probs)
```

```python
import functools
import math

import jax
import jax.numpy as jnp
from jax import lax
from jax.experimental import pallas as pl
from jax.experimental.pallas import tpu as pltpu
from jax.sharding import PartitionSpec as P

NC = 64
EPS = 1e-06
SHARP = 16.0
TEMPER = 4.0
GROUP = 4


def unit_kernel(own_ref, other_ref, out_ref):
    step = pl.program_id(0)

    def unit(ref):
        wide = ref[...].astype(jnp.float32)
        norm = jnp.sum(wide * wide, axis=-1, keepdims=True)
        out_ref[...] = (wide * lax.rsqrt(norm + EPS)).astype(jnp.bfloat16)

    half = pl.num_programs(0) // 2

    @pl.when(step < half)
    def _():
        unit(own_ref)

    @pl.when(step >= half)
    def _():
        unit(other_ref)


def unit_blocks(own, other):
    count, tokens, width = own.shape
    tile = 32
    half = count // tile
    return pl.pallas_call(
        unit_kernel,
        out_shape=jax.ShapeDtypeStruct((2 * count, tokens, width), jnp.bfloat16),
        grid=(2 * half,),
        in_specs=[
            pl.BlockSpec((tile, tokens, width), lambda i: (jnp.minimum(i, half - 1), 0, 0)),
            pl.BlockSpec((tile, tokens, width), lambda i: (jnp.maximum(i - half, 0), 0, 0)),
        ],
        out_specs=pl.BlockSpec((tile, tokens, width), lambda i: (i, 0, 0)),
        cost_estimate=pl.CostEstimate(
            flops=4 * own.size, bytes_accessed=8 * own.size, transcendentals=0
        ),
        name="unit_blocks",
    )(own, other)


def score_article(rows, base, count_ref, list_ref, query_ref, catalog_ref, out_ref, mass_ref):
    query = query_ref[0]
    wide = query.astype(jnp.float32)
    ones = jnp.ones((8, query.shape[1]), jnp.bfloat16)
    norm = lax.dot_general(
        ones,
        (wide * wide).astype(jnp.bfloat16),
        (((1,), (1,)), ((), ())),
        preferred_element_type=jnp.float32,
    )
    scale = lax.rsqrt(norm + EPS)[0:1] * (SHARP * math.log2(math.e))
    turned = query.T
    mass_ref[...] = jnp.ones_like(mass_ref)
    tokens = catalog_ref.shape[1]
    position = base + pl.program_id(0)
    count = count_ref[position]

    def some(step, carry):
        entries = [list_ref[position, step * GROUP + g] for g in range(GROUP)]
        blocks = jnp.concatenate([catalog_ref[e // 128] for e in entries], axis=0)
        sims = jnp.dot(blocks, turned, preferred_element_type=jnp.float32)
        grown = jnp.exp2(sims * scale)
        for g, e in enumerate(entries):
            mass_ref[pl.ds(e % 128, 1), :] = jnp.sum(
                grown[g * tokens : (g + 1) * tokens], axis=0, keepdims=True
            )
        return carry

    lax.fori_loop(0, (count + GROUP - 1) // GROUP, some, 0)
    logs = jnp.log(mass_ref[0:NC, :])
    out_ref[0] = lax.dot_general(
        jnp.full((8, logs.shape[1]), 1.0 / SHARP, jnp.float32),
        logs,
        (((1,), (1,)), ((), ())),
        precision=lax.Precision.HIGHEST,
        preferred_element_type=jnp.float32,
    )


def score_kernel(rows, count_ref, list_ref, first_ref, second_ref, catalog_ref, a_ref, b_ref, mass_ref):
    score_article(rows, 0, count_ref, list_ref, first_ref, catalog_ref, a_ref, mass_ref)
    score_article(rows, rows, count_ref, list_ref, second_ref, catalog_ref, b_ref, mass_ref)


def score_chunks(first, second, rows, begin, counts, lists, catalog):
    _, tokens, width = first.shape
    blocks, keys, _ = catalog.shape
    a, b = pl.pallas_call(
        functools.partial(score_kernel, rows),
        out_shape=[jax.ShapeDtypeStruct((rows, 8, NC), jnp.float32)] * 2,
        grid_spec=pltpu.PrefetchScalarGridSpec(
            num_scalar_prefetch=2,
            grid=(rows,),
            in_specs=[
                pl.BlockSpec((1, tokens, width), lambda i, *_: (i, 0, 0)),
                pl.BlockSpec((1, tokens, width), lambda i, *_: (i + begin, 0, 0)),
                pl.BlockSpec(memory_space=pltpu.VMEM),
            ],
            out_specs=[pl.BlockSpec((1, 8, NC), lambda i, *_: (i, 0, 0))] * 2,
            scratch_shapes=[pltpu.VMEM((NC + 8, tokens), jnp.float32)],
        ),
        compiler_params=pltpu.CompilerParams(vmem_limit_bytes=40 * 1024 * 1024),
        cost_estimate=pl.CostEstimate(
            flops=2 * 2 * rows * 8 * tokens * keys * width,
            bytes_accessed=2 * catalog.size,
            transcendentals=2 * rows * 8 * tokens * keys,
        ),
        name="score_chunks",
    )(counts, lists, first, second, catalog)
    return a[:, 0], b[:, 0]


def per_device(chips, ring, queries, cand_owner, cand_local, companies):
    articles = queries.shape[0]
    seqs = lax.axis_size("seq")
    arts = lax.axis_size("art")
    art, seq = lax.axis_index("art"), lax.axis_index("seq")
    chip, core = art // 2, art % 2
    blocks = companies.shape[0]
    mine = queries.reshape(articles, queries.shape[2], queries.shape[3])

    def turn(step):
        return [
            (2 * ring[i] + c, 2 * ring[(i + step) % chips] + c) for i in range(chips) for c in (0, 1)
        ]

    ahead = [mine]
    behind = [mine]
    half = chips // 2
    rows = articles // 2
    for _ in range(half - 1):
        ahead.append(lax.ppermute(ahead[-1], "art", turn(1)))
        behind.append(lax.ppermute(behind[-1], "art", turn(-1)))
    ahead.append(lax.ppermute(ahead[-1][:rows], "art", turn(1)))
    behind.append(lax.ppermute(behind[-1][rows:], "art", turn(-1)))

    other = lax.ppermute(companies, "art", [(i, i ^ 1) for i in range(arts)])
    catalog = unit_blocks(companies, other)

    ids = (cand_owner * blocks + cand_local).reshape(1, articles, NC)
    every = lax.all_to_all(
        jnp.broadcast_to(ids, (arts * seqs, articles, NC)),
        ("art", "seq"),
        split_axis=0,
        concat_axis=0,
        tiled=True,
    )
    every = every.reshape(chips, 2, articles, seqs, NC)
    needed = lax.dynamic_index_in_dim(
        lax.dynamic_index_in_dim(every, seq, 3, keepdims=False), core, 1, keepdims=False
    )
    order = jnp.array(ring, jnp.int32)
    spot = jnp.sum(jnp.where(order == chip, jnp.arange(chips), 0))
    needed = needed[jnp.array(ring)]
    needed = lax.dynamic_slice_in_dim(jnp.concatenate([needed, needed]), spot, chips)
    owners = needed // blocks
    here = owners // 2 == chip
    rank = jnp.cumsum(here.astype(jnp.int32), axis=-1) - 1
    counts = rank[..., -1] + 1
    entry = ((owners % 2 != core) * blocks + needed % blocks) * 128 + jnp.arange(NC)
    places = jnp.arange(NC)
    filled = jnp.sum(
        jnp.where(
            here[..., None, :] & (rank[..., None, :] == places[:, None]), entry[..., None, :], 0
        ),
        axis=-1,
    )
    lists = jnp.where(places < counts[..., None], filled, NC)

    def some(first, second, count, begin, j, k):
        ca, cb = counts[j][:count], counts[k][articles - count :]
        la, lb = lists[j][:count], lists[k][articles - count :]
        return score_chunks(
            first, second, count, begin, jnp.concatenate([ca, cb]), jnp.concatenate([la, lb]), catalog
        )

    scores = [None] * chips
    a, b = some(mine, mine, rows, rows, 0, 0)
    scores[0] = jnp.concatenate([a, b])
    for d in range(1, half):
        scores[chips - d], scores[d] = some(ahead[d], behind[d], articles, 0, chips - d, d)
    a, b = some(ahead[half], behind[half], rows, 0, half, half)
    scores[half] = jnp.concatenate([a, b])
    scores = jnp.stack(scores)
    scores = lax.dynamic_slice_in_dim(jnp.concatenate([scores, scores]), chips - spot, chips)
    back = [0] * chips
    for i, c in enumerate(ring):
        back[c] = i
    scores = scores[jnp.array(back)]
    scores = jnp.where(
        (jnp.arange(2) == core)[None, :, None, None], scores[:, None], 0.0
    ).reshape(arts * seqs, articles // seqs, NC)
    parts = lax.all_to_all(scores, ("art", "seq"), split_axis=0, concat_axis=0, tiled=True)
    parts = parts.reshape(arts, seqs, articles // seqs, NC).sum(0)
    score = parts.transpose(1, 0, 2).reshape(articles, NC)
    relevance = score - jnp.mean(score, axis=-1, keepdims=True)
    weights = jnp.exp(TEMPER * relevance)
    probs = weights / jnp.sum(weights, axis=-1, keepdims=True)
    return (relevance, probs)


def solution(mesh):
    arts, seqs = mesh.shape["art"], mesh.shape["seq"]
    chips = arts // 2
    wide = math.gcd(seqs, chips)
    deep = chips // wide
    ring = []
    for y in range(wide):
        for z in range(deep) if y % 2 == 0 else reversed(range(deep)):
            ring.append(z * wide + y)
    placed = (
        P("art", "seq", None, None),
        P(("art", "seq"), None, None),
        P(("art", "seq"), None, None),
        P("art", None, None),
    )
    return jax.shard_map(
        functools.partial(per_device, chips, tuple(ring)),
        mesh=mesh,
        in_specs=placed,
        out_specs=(P(("art", "seq"), None), P(("art", "seq"), None)),
        check_vma=False,
    )
```

```python
import functools
import math

import jax
import jax.numpy as jnp
from jax import lax
from jax.experimental import pallas as pl
from jax.experimental.pallas import tpu as pltpu
from jax.sharding import PartitionSpec as P

NC = 64
EPS = 1e-06
SHARP = 16.0
TEMPER = 4.0
GROUP = 4
UNROLL = 12
LAST = (((1,), (1,)), ((), ()))


def unit_kernel(blocks_ref, out_ref):
    count, tokens, width = blocks_ref.shape

    def some(i, carry):
        wide = blocks_ref[pl.ds(2 * i, 2)].astype(jnp.float32)
        norm = jnp.sum(wide * wide, axis=-1, keepdims=True)
        out_ref[pl.ds(2 * i, 2)] = (wide * lax.rsqrt(norm + EPS)).astype(jnp.bfloat16)
        return carry

    lax.fori_loop(0, count // 2, some, 0, unroll=16)


def unit_blocks(blocks):
    return pl.pallas_call(
        unit_kernel,
        out_shape=jax.ShapeDtypeStruct(blocks.shape, jnp.bfloat16),
        in_specs=[pl.BlockSpec(memory_space=pltpu.VMEM)],
        out_specs=pl.BlockSpec(memory_space=pltpu.VMEM),
        compiler_params=pltpu.CompilerParams(vmem_limit_bytes=32 * 1024 * 1024),
        cost_estimate=pl.CostEstimate(flops=1, bytes_accessed=1, transcendentals=0),
        name="unit_blocks",
    )(blocks)


def mask(m):
    return m.astype(jnp.float32).astype(jnp.bfloat16)


def plan_rows(chips, articles):
    entries = -(-(articles * NC + chips * articles * (GROUP - 1)) // 128)
    return entries, -(-(3 * entries + 1) // 16) * 16


def pack_kernel(chips, blocks, me_ref, *refs):
    id_refs, query_ref, out_ref = refs[:-2], refs[-2], refs[-1]
    seqs = len(id_refs)
    core, seq = me_ref[1], me_ref[2]
    per_home, width = id_refs[0].shape
    rows = query_ref.shape[0]
    out_ref[0:rows, :] = query_ref[...]

    lane = lax.broadcasted_iota(jnp.int32, (per_home, width), 1)
    ids = jnp.zeros((per_home, width), jnp.int32)
    for d in range(seqs):
        table = id_refs[d][...]
        for p in range(seqs):
            k = (p + seqs - d) % seqs
            turned = table if k == p else pltpu.roll(table, (k - p) % seqs * NC, 1)
            ids = jnp.where((seq == p) & (lane // NC == k), turned, ids)
    ids = jnp.concatenate([ids[i : i + 1] for i in range(per_home)], axis=1)
    lanes = per_home * width
    articles = lanes // NC
    owner, local = ids // blocks, ids % blocks
    other = jnp.where(owner % 2 != core, 1, 0)
    here = owner // 2 == lax.broadcasted_iota(jnp.int32, (chips, lanes), 0)
    hot = mask(here)
    a = lax.broadcasted_iota(jnp.int32, (lanes, lanes), 0)
    b = lax.broadcasted_iota(jnp.int32, (lanes, lanes), 1)
    same = a // NC == b // NC
    rank = jnp.dot(hot, mask(same & (a <= b)), preferred_element_type=jnp.float32)
    amount = jnp.dot(hot, mask(same), preferred_element_type=jnp.float32).astype(jnp.int32)
    groups = (amount + (GROUP - 1)) // GROUP
    lead = lax.broadcasted_iota(jnp.int32, (chips, lanes), 1) % NC == 0
    tops = jnp.where(lead, groups, 0).astype(jnp.float32)
    ahead = jnp.dot(
        tops.astype(jnp.bfloat16), mask(a // NC < b // NC), preferred_element_type=jnp.float32
    )
    totals = jnp.sum(tops, axis=1, keepdims=True)
    lane = lax.broadcasted_iota(jnp.int32, (chips, 128), 1)
    before = lax.broadcasted_iota(jnp.int32, (chips, 128), 0) < lane % NC
    starts = jnp.sum(jnp.where(before, totals, 0.0), axis=0, keepdims=True).astype(jnp.int32)
    starts = jnp.where(lane[0:1] < NC, starts // 16, starts % 16).astype(jnp.float32)
    fence = mask(
        lax.broadcasted_iota(jnp.int32, (chips, chips), 1)
        < lax.broadcasted_iota(jnp.int32, (chips, chips), 0)
    )
    base = jnp.dot(fence, tops.astype(jnp.bfloat16), preferred_element_type=jnp.float32)
    base = jnp.sum(base, axis=1, keepdims=True)
    spot = jnp.where(here, GROUP * (base + ahead) + rank - 1.0, 0.0)
    spot = jnp.sum(spot, axis=0, keepdims=True).astype(jnp.int32)
    lane = lax.broadcasted_iota(jnp.int32, (1, lanes), 1)
    article = lane // NC % seqs * per_home + lane // width
    kinds = lax.broadcasted_iota(jnp.int32, (8, lanes), 0)
    fields = jnp.ones((8, lanes), jnp.int32)
    for k, row in enumerate((local, other * 128 + lane % NC, article)):
        fields = jnp.where(kinds == k, row, fields)
    entries, extra = plan_rows(chips, articles)
    slots = lax.broadcasted_iota(jnp.int32, (entries * 128, lanes), 0)
    got = lax.dot_general(
        fields.astype(jnp.float32).astype(jnp.bfloat16),
        mask(slots == spot),
        LAST,
        preferred_element_type=jnp.float32,
    )
    code = jnp.where(got[3:4] > 0.5, got[1:2], float(NC))
    lists = jnp.concatenate([got[0:1], code, got[2:3]], axis=1)
    lists = [lists[:, i * 128 : (i + 1) * 128] for i in range(3 * entries)]
    lists += [starts, jnp.zeros((extra - 3 * entries - 1, 128), jnp.float32)]
    out_ref[rows : rows + extra, :] = jnp.concatenate(lists, axis=0).astype(jnp.bfloat16)


def pack_stream(me, ids, query, chips, blocks):
    vmem = pl.BlockSpec(memory_space=pltpu.VMEM)
    articles = len(ids) * ids[0].shape[0]
    rows = query.shape[0] + plan_rows(chips, articles)[1]
    return pl.pallas_call(
        functools.partial(pack_kernel, chips, blocks),
        out_shape=jax.ShapeDtypeStruct((rows, query.shape[1]), jnp.bfloat16),
        in_specs=[pl.BlockSpec(memory_space=pltpu.SMEM)] + [vmem] * (len(ids) + 1),
        out_specs=vmem,
        compiler_params=pltpu.CompilerParams(vmem_limit_bytes=32 * 1024 * 1024),
        cost_estimate=pl.CostEstimate(flops=1, bytes_accessed=1, transcendentals=0),
        name="pack_stream",
    )(me, *ids, query)


def score_kernel(dims, me_ref, *refs):
    plans, others, seqs, blocks, wide, deep = dims
    chips = wide * deep
    pair_refs, refs = refs[: 2 * plans], refs[2 * plans :]
    other_refs, refs = refs[:others], refs[others:]
    own_ref, other_ref, *refs = refs
    out_refs = refs[:-6]
    turned_ref, scale_ref, mass_ref, words_ref, lists_ref, sems = refs[-6:]
    articles = turned_ref.shape[0] // plans
    tokens = mass_ref.shape[1]
    keys = own_ref.shape[1]
    half = mass_ref.shape[0] // plans
    entries, extra = plan_rows(chips, articles)
    bits = (2 * blocks - 1).bit_length()
    begin = articles // 2 * tokens

    copies = []
    for p in range(plans):
        rows = pair_refs[2 * p + 1][begin : begin + extra, :].astype(jnp.float32).astype(jnp.int32)
        local, code, article, starts = (rows[k * entries : (k + 1) * entries] for k in range(4))
        place = code % 128
        row = jnp.where(place < NC, article * NC + place, articles * NC)
        word = local + blocks * (code // 128) + 2 * blocks * row + (1 << 20) * article
        words_ref[p, 0:entries, :] = word
        words_ref[p, entries : entries + 1, :] = starts[0:1]
        copy = pltpu.make_async_copy(words_ref.at[p], lists_ref.at[p], sems.at[p])
        copy.start()
        copies.append(copy)

    for p, ref in enumerate(pair_refs):

        def prepare(i, carry, p=p, ref=ref):
            query = ref[pl.ds(pl.multiple_of(i * tokens, tokens), tokens), :]
            wide = query.astype(jnp.float32)
            norm = lax.dot_general(
                jnp.ones((8, query.shape[1]), jnp.bfloat16),
                (wide * wide).astype(jnp.bfloat16),
                LAST,
                preferred_element_type=jnp.float32,
            )
            at = p * (articles // 2) + i
            scale_ref[at] = lax.rsqrt(norm + EPS) * (SHARP * math.log2(math.e))
            turned_ref[at] = query.T
            return carry

        lax.fori_loop(0, articles // 2, prepare, 0, unroll=2)
    mass_ref[...] = jnp.ones_like(mass_ref)
    for copy in copies:
        copy.wait()

    chip = me_ref[0]
    begins = []
    counts = []
    for p in range(plans):
        low = lists_ref[p, entries, chip] * 16 + lists_ref[p, entries, NC + chip]
        high = lists_ref[p, entries, chip + 1] * 16 + lists_ref[p, entries, NC + chip + 1]
        begins.append(low)
        counts.append(high - low)
    total = sum(counts)

    def task(k):
        k = jnp.minimum(k, total - 1)
        if plans == 1:
            late, at = 0, (k + begins[0]) * GROUP
        else:
            late = (k >= counts[0]).astype(jnp.int32)
            at = (k + begins[0] + late * (begins[1] - begins[0] - counts[0])) * GROUP
        at = jnp.maximum(at, 0)
        line, spot = lax.shift_right_logical(at, 7), at & 127
        words = [lists_ref[late, line, spot + g] for g in range(GROUP)]
        article = lax.shift_right_logical(words[0], 20) + late * articles
        rows = [(lax.shift_right_logical(w, bits) & 2047) + late * half for w in words]
        return article, [w & (2 * blocks - 1) for w in words], rows

    def block(c):
        spot = c & (blocks - 1)
        return jnp.where(c >= blocks, other_ref[spot], own_ref[spot])

    def some(step, carry):
        for u in range(UNROLL):
            article, picks, rows = task(step * UNROLL + u)
            chosen = jnp.concatenate([block(c) for c in picks], axis=0)
            sims = jnp.dot(chosen, turned_ref[article], preferred_element_type=jnp.float32)
            grown = jnp.exp2(sims * scale_ref[article][0:1])
            for g, row in enumerate(rows):
                mass_ref[pl.ds(row, 1), :] = jnp.sum(
                    grown[g * keys : (g + 1) * keys], axis=0, keepdims=True
                )
        return carry

    lax.fori_loop(0, (total + UNROLL - 1) // UNROLL, some, 0)

    per_home = articles // seqs
    ones = jnp.ones((8, tokens), jnp.bfloat16)
    for p in range(plans):
        for i in range(articles):
            logs = jnp.log2(mass_ref[p * half + i * NC : p * half + (i + 1) * NC, :])
            high = logs.astype(jnp.bfloat16)
            low = (logs - high.astype(jnp.float32)).astype(jnp.bfloat16)
            sums = lax.dot_general(
                ones, high, LAST, preferred_element_type=jnp.float32
            ) + lax.dot_general(ones, low, LAST, preferred_element_type=jnp.float32)
            out_refs[p][i : i + 1, 0:NC] = sums[0:1] * (math.log(2) / SHARP)
    if not others:
        return

    spread_ref = out_refs[-1]
    spread_ref[...] = jnp.zeros_like(spread_ref)
    block_rows = spread_ref.shape[0] // (2 * chips * seqs)
    side, rest = chip & (wide - 1), chip >> (wide.bit_length() - 1)
    place = side * deep + jnp.where(side & 1 == 0, rest, deep - 1 - rest)
    spots = [0] + [x for d in range(1, chips // 2) for x in (-d, d)] + [chips // 2]
    for spot, ref in zip(spots, [*other_refs, out_refs[0]]):
        at = (place + spot + chips) & (chips - 1)
        side, rest = at >> (deep.bit_length() - 1), at & (deep - 1)
        home = jnp.where(side & 1 == 0, rest, deep - 1 - rest) * wide + side
        for k in range(seqs):
            peer = (2 * home + me_ref[1]) * seqs + k
            rows = pl.ds(pl.multiple_of(peer * block_rows, 8), per_home)
            spread_ref[rows, :] = ref[k * per_home : (k + 1) * per_home, :]


def score_chunks(me, pairs, others, own, other, tokens, wide, deep, seqs):
    chips = wide * deep
    plans = len(pairs)
    blocks, keys, width = own.shape
    articles = 2 * pairs[0][0].shape[0] // tokens
    shapes = [jax.ShapeDtypeStruct((articles, 128), jnp.float32)] * plans
    if others:
        rows = -(-(articles // seqs) // 8) * 8 * 2 * chips * seqs
        shapes.append(jax.ShapeDtypeStruct((rows, 128), jnp.float32))
    lines = -(-(plan_rows(chips, articles)[0] + 1) // 8) * 8
    work = plans * articles * 8
    smem, vmem = pl.BlockSpec(memory_space=pltpu.SMEM), pl.BlockSpec(memory_space=pltpu.VMEM)
    return pl.pallas_call(
        functools.partial(score_kernel, (plans, len(others), seqs, blocks, wide, deep)),
        out_shape=shapes,
        in_specs=[smem] + [vmem] * (2 * plans + len(others) + 2),
        out_specs=[vmem] * len(shapes),
        scratch_shapes=[
            pltpu.VMEM((plans * articles, width, tokens), jnp.bfloat16),
            pltpu.VMEM((plans * articles, 8, tokens), jnp.float32),
            pltpu.VMEM((plans * (articles * NC + 8), tokens), jnp.float32),
            pltpu.VMEM((plans, lines, 128), jnp.int32),
            pltpu.SMEM((plans, lines, 128), jnp.int32),
            pltpu.SemaphoreType.DMA((plans,)),
        ],
        compiler_params=pltpu.CompilerParams(vmem_limit_bytes=32 * 1024 * 1024),
        cost_estimate=pl.CostEstimate(
            flops=2 * work * tokens * keys * width,
            bytes_accessed=4 * own.size,
            transcendentals=work * tokens * keys,
        ),
        name="score_chunks",
    )(me, *[x for pair in pairs for x in pair], *others, own, other)


def close_kernel(seqs, parts_ref, relevance_ref, probs_ref, score_ref):
    peers = parts_ref.shape[0]
    rows = relevance_ref.shape[0] // seqs
    for d in range(seqs):
        part = parts_ref[d]
        for j in range(d + seqs, peers, seqs):
            part = part + parts_ref[j]
        for i in range(rows):
            score_ref[i * seqs + d : i * seqs + d + 1, :] = part[i : i + 1]
    score = score_ref[:, 0:NC]
    relevance = score - jnp.mean(score, axis=-1, keepdims=True)
    weights = jnp.exp(TEMPER * relevance)
    relevance_ref[...] = relevance
    probs_ref[...] = weights / jnp.sum(weights, axis=-1, keepdims=True)


def close(parts, articles, seqs):
    vmem = pl.BlockSpec(memory_space=pltpu.VMEM)
    return pl.pallas_call(
        functools.partial(close_kernel, seqs),
        out_shape=[jax.ShapeDtypeStruct((articles, NC), jnp.float32)] * 2,
        in_specs=[vmem],
        out_specs=[vmem] * 2,
        scratch_shapes=[pltpu.VMEM((articles, 128), jnp.float32)],
        name="close",
    )(parts)


def per_device(wide, deep, queries, cand_owner, cand_local, companies):
    articles = queries.shape[0]
    seqs, arts = lax.axis_size("seq"), lax.axis_size("art")
    art, seq = lax.axis_index("art"), lax.axis_index("seq")
    chips = wide * deep
    half = chips // 2
    per_home = articles // seqs
    blocks = companies.shape[0]
    tokens = queries.shape[2]
    mine = queries.reshape(articles * tokens, queries.shape[3])
    ring = []
    for y in range(wide):
        for z in range(deep) if y % 2 == 0 else reversed(range(deep)):
            ring.append(z * wide + y)

    def turn(step, across=0):
        return [
            (
                (2 * ring[i] + c) * seqs + s,
                (2 * ring[(i + step) % chips] + c) * seqs + (s + across) % seqs,
            )
            for i in range(chips)
            for c in range(2)
            for s in range(seqs)
        ]

    def send(array, step, across=0):
        return lax.ppermute(array, ("art", "seq"), turn(step, across))

    cut = articles // 2 * tokens
    one = mine[:cut]
    ahead, behind = [[one, None]], [[one, None]]
    first = [send(one, 1), send(one, -1)]

    ids = (cand_owner * blocks + cand_local).reshape(per_home, seqs * NC)
    ids = [ids] + [send(ids, 0, d) for d in range(1, seqs)]
    me = jnp.stack([art // 2, art % 2, seq]).astype(jnp.int32)
    two = pack_stream(me, ids, mine[cut:], chips, blocks)
    second = [send(two, 1), send(two, -1)]
    ahead.append([first[0], second[0]])
    behind.append([first[1], second[1]])
    own = unit_blocks(companies)
    other = unit_blocks(lax.ppermute(companies, "art", [(i, i ^ 1) for i in range(arts)]))

    def score(*pairs, others=()):
        return score_chunks(me, pairs, others, own, other, tokens, wide, deep, seqs)

    done = score((one, two))
    early = list(done)
    for d in range(1, half):
        for side in (ahead, behind):
            side[d] = [lax.optimization_barrier((x, done[0]))[0] for x in side[d]]
        if d + 1 < half:
            ahead.append([send(x, 1) for x in ahead[d]])
            behind.append([send(x, -1) for x in behind[d]])
        else:
            last = (send(ahead[d][0], 1), send(behind[d][1], -1))
        done = score(ahead[d], behind[d])
        early += done
    spread = score(last, others=early)[1]
    parts = lax.all_to_all(spread, ("art", "seq"), split_axis=0, concat_axis=0, tiled=True)
    return tuple(close(parts.reshape(arts * seqs, -1, 128), articles, seqs))


def solution(mesh):
    chips = mesh.shape["art"] // 2
    wide = math.gcd(mesh.shape["seq"], chips)
    placed = (
        P("art", "seq", None, None),
        P(("art", "seq"), None, None),
        P(("art", "seq"), None, None),
        P("art", None, None),
    )
    return jax.shard_map(
        functools.partial(per_device, wide, chips // wide),
        mesh=mesh,
        in_specs=placed,
        out_specs=(P(("art", "seq"), None), P(("art", "seq"), None)),
        check_vma=False,
    )
```

```python
import functools
import math

import jax
import jax.numpy as jnp
from jax import lax
from jax.experimental import pallas as pl
from jax.experimental.pallas import tpu as pltpu
from jax.sharding import PartitionSpec as P

NC = 64
EPS = 1e-06
SHARP = 16.0
TEMPER = 4.0
GROUP = 4
UCOST = 4000000000
SCOST = 2.0
UNROLL = 16
PREP = 3
LAST = (((1,), (1,)), ((), ()))


def unit_kernel(parts, blocks_ref, out_ref, held_ref, sems):
    part = blocks_ref.shape[0] // parts
    copies = []
    for p in range(parts):
        rows = pl.ds(p * part, part)
        copies.append(pltpu.make_async_copy(blocks_ref.at[rows], held_ref.at[rows], sems.at[p]))
        copies[-1].start()
    for p in range(parts):
        copies[p].wait()

        def some(i, carry, p=p):
            rows = pl.ds(p * part + 2 * i, 2)
            wide = held_ref[rows].astype(jnp.float32)
            norm = jnp.sum(wide * wide, axis=-1, keepdims=True)
            out_ref[rows] = (wide * lax.rsqrt(norm + EPS)).astype(jnp.bfloat16)
            return carry

        lax.fori_loop(0, part // 2, some, 0, unroll=16)


def unit_blocks(blocks):
    parts = 4
    return pl.pallas_call(
        functools.partial(unit_kernel, parts),
        out_shape=jax.ShapeDtypeStruct(blocks.shape, jnp.bfloat16),
        in_specs=[pl.BlockSpec(memory_space=pltpu.HBM)],
        out_specs=pl.BlockSpec(memory_space=pltpu.VMEM),
        scratch_shapes=[
            pltpu.VMEM(blocks.shape, jnp.bfloat16),
            pltpu.SemaphoreType.DMA((parts,)),
        ],
        compiler_params=pltpu.CompilerParams(vmem_limit_bytes=32 * 1024 * 1024),
        cost_estimate=pl.CostEstimate(flops=UCOST, bytes_accessed=1, transcendentals=0),
        name="unit_blocks",
    )(blocks)


def mask(m):
    return m.astype(jnp.float32).astype(jnp.bfloat16)


def plan_rows(chips, articles):
    entries = -(-(articles * NC + chips * articles * (GROUP - 1)) // 128)
    return entries, -(-(3 * entries + 1) // 16) * 16


def pack_kernel(chips, blocks, me_ref, *refs):
    id_refs, query_ref, out_ref = refs[:-2], refs[-2], refs[-1]
    seqs = len(id_refs)
    core, seq = me_ref[1], me_ref[2]
    per_home, width = id_refs[0].shape
    rows = query_ref.shape[0]
    out_ref[0:rows, :] = query_ref[...]

    lane = lax.broadcasted_iota(jnp.int32, (per_home, width), 1)
    ids = jnp.zeros((per_home, width), jnp.int32)
    for d in range(seqs):
        table = id_refs[d][...]
        for p in range(seqs):
            k = (p + seqs - d) % seqs
            turned = table if k == p else pltpu.roll(table, (k - p) % seqs * NC, 1)
            ids = jnp.where((seq == p) & (lane // NC == k), turned, ids)
    ids = jnp.concatenate([ids[i : i + 1] for i in range(per_home)], axis=1)
    lanes = per_home * width
    articles = lanes // NC
    owner, local = ids // blocks, ids % blocks
    other = jnp.where(owner % 2 != core, 1, 0)
    here = owner // 2 == lax.broadcasted_iota(jnp.int32, (chips, lanes), 0)
    hot = mask(here)
    a = lax.broadcasted_iota(jnp.int32, (lanes, lanes), 0)
    b = lax.broadcasted_iota(jnp.int32, (lanes, lanes), 1)
    same = a // NC == b // NC
    rank = jnp.dot(hot, mask(same & (a <= b)), preferred_element_type=jnp.float32)
    amount = jnp.dot(hot, mask(same), preferred_element_type=jnp.float32).astype(jnp.int32)
    groups = (amount + (GROUP - 1)) // GROUP
    lead = lax.broadcasted_iota(jnp.int32, (chips, lanes), 1) % NC == 0
    tops = jnp.where(lead, groups, 0).astype(jnp.float32)
    ahead = jnp.dot(
        tops.astype(jnp.bfloat16), mask(a // NC < b // NC), preferred_element_type=jnp.float32
    )
    totals = jnp.sum(tops, axis=1, keepdims=True)
    lane = lax.broadcasted_iota(jnp.int32, (chips, 128), 1)
    before = lax.broadcasted_iota(jnp.int32, (chips, 128), 0) < lane % NC
    starts = jnp.sum(jnp.where(before, totals, 0.0), axis=0, keepdims=True).astype(jnp.int32)
    starts = jnp.where(lane[0:1] < NC, starts // 16, starts % 16).astype(jnp.float32)
    fence = mask(
        lax.broadcasted_iota(jnp.int32, (chips, chips), 1)
        < lax.broadcasted_iota(jnp.int32, (chips, chips), 0)
    )
    base = jnp.dot(fence, tops.astype(jnp.bfloat16), preferred_element_type=jnp.float32)
    base = jnp.sum(base, axis=1, keepdims=True)
    spot = jnp.where(here, GROUP * (base + ahead) + rank - 1.0, 0.0)
    spot = jnp.sum(spot, axis=0, keepdims=True).astype(jnp.int32)
    lane = lax.broadcasted_iota(jnp.int32, (1, lanes), 1)
    article = lane // NC % seqs * per_home + lane // width
    kinds = lax.broadcasted_iota(jnp.int32, (8, lanes), 0)
    fields = jnp.ones((8, lanes), jnp.int32)
    for k, row in enumerate((local, other * 128 + lane % NC, article)):
        fields = jnp.where(kinds == k, row, fields)
    entries, extra = plan_rows(chips, articles)
    slots = lax.broadcasted_iota(jnp.int32, (entries * 128, lanes), 0)
    got = lax.dot_general(
        fields.astype(jnp.float32).astype(jnp.bfloat16),
        mask(slots == spot),
        LAST,
        preferred_element_type=jnp.float32,
    )
    code = jnp.where(got[3:4] > 0.5, got[1:2], float(NC))
    lists = jnp.concatenate([got[0:1], code, got[2:3]], axis=1)
    lists = [lists[:, i * 128 : (i + 1) * 128] for i in range(3 * entries)]
    lists += [starts, jnp.zeros((extra - 3 * entries - 1, 128), jnp.float32)]
    out_ref[rows : rows + extra, :] = jnp.concatenate(lists, axis=0).astype(jnp.bfloat16)


def pack_stream(me, ids, query, chips, blocks):
    vmem = pl.BlockSpec(memory_space=pltpu.VMEM)
    articles = len(ids) * ids[0].shape[0]
    half = query.shape[0] // 2
    rows = half + plan_rows(chips, articles)[1]
    return pl.pallas_call(
        functools.partial(pack_kernel, chips, blocks),
        out_shape=jax.ShapeDtypeStruct((rows, query.shape[1]), jnp.bfloat16),
        grid=(1,),
        in_specs=[pl.BlockSpec(memory_space=pltpu.SMEM)]
        + [vmem] * len(ids)
        + [pl.BlockSpec((half, query.shape[1]), lambda i: (1, 0))],
        out_specs=vmem,
        compiler_params=pltpu.CompilerParams(vmem_limit_bytes=32 * 1024 * 1024),
        cost_estimate=pl.CostEstimate(flops=1, bytes_accessed=1, transcendentals=0),
        name="pack_stream",
    )(me, *ids, query)


def score_kernel(dims, me_ref, *refs):
    plans, others, seqs, blocks, wide, deep = dims
    chips = wide * deep
    pair_refs, refs = refs[: 2 * plans], refs[2 * plans :]
    other_refs, refs = refs[:others], refs[others:]
    own_ref, other_ref, *refs = refs
    out_refs = refs[:-6]
    turned_ref, scale_ref, mass_ref, words_ref, lists_ref, sems = refs[-6:]
    articles = turned_ref.shape[0] // plans
    tokens = mass_ref.shape[1]
    keys = own_ref.shape[1]
    half = mass_ref.shape[0] // plans
    entries, extra = plan_rows(chips, articles)
    bits = (2 * blocks - 1).bit_length()
    begin = articles // 2 * tokens

    copies = []
    for p in range(plans):
        rows = pair_refs[2 * p + 1][begin : begin + extra, :].astype(jnp.float32).astype(jnp.int32)
        local, code, article, starts = (rows[k * entries : (k + 1) * entries] for k in range(4))
        place = code % 128
        row = jnp.where(place < NC, article * NC + place, articles * NC)
        word = local + blocks * (code // 128) + 2 * blocks * row + (1 << 20) * article
        words_ref[p, 0:entries, :] = word
        words_ref[p, entries : entries + 1, :] = starts[0:1]
        copy = pltpu.make_async_copy(words_ref.at[p], lists_ref.at[p], sems.at[p])
        copy.start()
        copies.append(copy)

    def prepare(i, carry):
        for p, ref in enumerate(pair_refs):
            query = ref[pl.ds(pl.multiple_of(i * tokens, tokens), tokens), :]
            wide = query.astype(jnp.float32)
            norm = lax.dot_general(
                jnp.ones((8, query.shape[1]), jnp.bfloat16),
                (wide * wide).astype(jnp.bfloat16),
                LAST,
                preferred_element_type=jnp.float32,
            )
            at = p * (articles // 2) + i
            scale_ref[at] = lax.rsqrt(norm + EPS) * (SHARP * math.log2(math.e))
            turned_ref[at] = query.T
        return carry

    lax.fori_loop(0, articles // 2, prepare, 0, unroll=PREP)
    mass_ref[...] = jnp.ones_like(mass_ref)
    for copy in copies:
        copy.wait()

    chip = me_ref[0]
    begins = []
    counts = []
    for p in range(plans):
        low = lists_ref[p, entries, chip] * 16 + lists_ref[p, entries, NC + chip]
        high = lists_ref[p, entries, chip + 1] * 16 + lists_ref[p, entries, NC + chip + 1]
        begins.append(low)
        counts.append(high - low)
    total = sum(counts)

    def task(k):
        k = jnp.minimum(k, total - 1)
        if plans == 1:
            late, at = 0, (k + begins[0]) * GROUP
        else:
            late = (k >= counts[0]).astype(jnp.int32)
            at = (k + begins[0] + late * (begins[1] - begins[0] - counts[0])) * GROUP
        at = jnp.maximum(at, 0)
        line, spot = lax.shift_right_logical(at, 7), at & 127
        words = [lists_ref[late, line, spot + g] for g in range(GROUP)]
        article = lax.shift_right_logical(words[0], 20) + late * articles
        rows = [(lax.shift_right_logical(w, bits) & 2047) + late * half for w in words]
        return article, [w & (2 * blocks - 1) for w in words], rows

    def block(c):
        spot = c & (blocks - 1)
        return jnp.where(c >= blocks, other_ref[spot], own_ref[spot])

    def some(step, carry):
        for u in range(UNROLL):
            article, picks, rows = task(step * UNROLL + u)
            chosen = jnp.concatenate([block(c) for c in picks], axis=0)
            sims = jnp.dot(chosen, turned_ref[article], preferred_element_type=jnp.float32)
            grown = jnp.exp2(sims * scale_ref[article][0:1])
            for g, row in enumerate(rows):
                mass_ref[pl.ds(row, 1), :] = jnp.sum(
                    grown[g * keys : (g + 1) * keys], axis=0, keepdims=True
                )
        return carry

    lax.fori_loop(0, (total + UNROLL - 1) // UNROLL, some, 0)

    per_home = articles // seqs
    lane = lax.broadcasted_iota(jnp.int32, (NC, 128), 1)
    for p in range(plans):
        sums = jnp.zeros((NC, 128), jnp.float32)
        for i in range(articles):
            logs = jnp.log2(mass_ref[p * half + i * NC : p * half + (i + 1) * NC, :])
            sums = jnp.where(lane == i, jnp.sum(logs, axis=1, keepdims=True), sums)
        out_refs[p][:, 0:NC] = (sums * (math.log(2) / SHARP)).T[0:articles]
    if not others:
        return

    spread_ref = out_refs[-1]
    spread_ref[...] = jnp.zeros_like(spread_ref)
    block_rows = spread_ref.shape[0] // (2 * chips * seqs)
    side, rest = chip & (wide - 1), chip >> (wide.bit_length() - 1)
    place = side * deep + jnp.where(side & 1 == 0, rest, deep - 1 - rest)
    spots = [0] + [x for d in range(1, chips // 2) for x in (-d, d)] + [chips // 2]
    for spot, ref in zip(spots, [*other_refs, out_refs[0]]):
        at = (place + spot + chips) & (chips - 1)
        side, rest = at >> (deep.bit_length() - 1), at & (deep - 1)
        home = jnp.where(side & 1 == 0, rest, deep - 1 - rest) * wide + side
        for k in range(seqs):
            peer = (2 * home + me_ref[1]) * seqs + k
            rows = pl.ds(pl.multiple_of(peer * block_rows, 8), per_home)
            spread_ref[rows, :] = ref[k * per_home : (k + 1) * per_home, :]


def score_chunks(me, pairs, others, own, other, tokens, wide, deep, seqs):
    chips = wide * deep
    plans = len(pairs)
    blocks, keys, width = own.shape
    articles = 2 * pairs[0][0].shape[0] // tokens
    shapes = [jax.ShapeDtypeStruct((articles, 128), jnp.float32)] * plans
    if others:
        rows = -(-(articles // seqs) // 8) * 8 * 2 * chips * seqs
        shapes.append(jax.ShapeDtypeStruct((rows, 128), jnp.float32))
    lines = -(-(plan_rows(chips, articles)[0] + 1) // 8) * 8
    work = plans * articles * 8
    smem, vmem = pl.BlockSpec(memory_space=pltpu.SMEM), pl.BlockSpec(memory_space=pltpu.VMEM)
    return pl.pallas_call(
        functools.partial(score_kernel, (plans, len(others), seqs, blocks, wide, deep)),
        out_shape=shapes,
        in_specs=[smem] + [vmem] * (2 * plans + len(others) + 2),
        out_specs=[vmem] * len(shapes),
        scratch_shapes=[
            pltpu.VMEM((plans * articles, width, tokens), jnp.bfloat16),
            pltpu.VMEM((plans * articles, 8, tokens), jnp.float32),
            pltpu.VMEM((plans * (articles * NC + 8), tokens), jnp.float32),
            pltpu.VMEM((plans, lines, 128), jnp.int32),
            pltpu.SMEM((plans, lines, 128), jnp.int32),
            pltpu.SemaphoreType.DMA((plans,)),
        ],
        compiler_params=pltpu.CompilerParams(vmem_limit_bytes=32 * 1024 * 1024),
        cost_estimate=pl.CostEstimate(
            flops=int(SCOST * work * tokens * keys * width),
            bytes_accessed=4 * own.size,
            transcendentals=int(SCOST / 2 * work * tokens * keys),
        ),
        name="score_chunks",
    )(me, *[x for pair in pairs for x in pair], *others, own, other)


def close_kernel(seqs, parts_ref, relevance_ref, probs_ref, score_ref):
    peers = parts_ref.shape[0]
    rows = relevance_ref.shape[0] // seqs
    for d in range(seqs):
        part = parts_ref[d]
        for j in range(d + seqs, peers, seqs):
            part = part + parts_ref[j]
        for i in range(rows):
            score_ref[i * seqs + d : i * seqs + d + 1, :] = part[i : i + 1]
    score = score_ref[:, 0:NC]
    relevance = score - jnp.mean(score, axis=-1, keepdims=True)
    weights = jnp.exp(TEMPER * relevance)
    relevance_ref[...] = relevance
    probs_ref[...] = weights / jnp.sum(weights, axis=-1, keepdims=True)


def close(parts, articles, seqs):
    vmem = pl.BlockSpec(memory_space=pltpu.VMEM)
    return pl.pallas_call(
        functools.partial(close_kernel, seqs),
        out_shape=[jax.ShapeDtypeStruct((articles, NC), jnp.float32)] * 2,
        in_specs=[vmem],
        out_specs=[vmem] * 2,
        scratch_shapes=[pltpu.VMEM((articles, 128), jnp.float32)],
        name="close",
    )(parts)


def per_device(wide, deep, queries, cand_owner, cand_local, companies):
    articles = queries.shape[0]
    seqs, arts = lax.axis_size("seq"), lax.axis_size("art")
    art, seq = lax.axis_index("art"), lax.axis_index("seq")
    chips = wide * deep
    half = chips // 2
    per_home = articles // seqs
    blocks = companies.shape[0]
    tokens = queries.shape[2]
    mine = queries.reshape(articles * tokens, queries.shape[3])
    ring = []
    for y in range(wide):
        for z in range(deep) if y % 2 == 0 else reversed(range(deep)):
            ring.append(z * wide + y)

    def turn(step, across=0):
        return [
            (
                (2 * ring[i] + c) * seqs + s,
                (2 * ring[(i + step) % chips] + c) * seqs + (s + across) % seqs,
            )
            for i in range(chips)
            for c in range(2)
            for s in range(seqs)
        ]

    def send(array, step, across=0):
        return lax.ppermute(array, ("art", "seq"), turn(step, across))

    cut = articles // 2 * tokens
    one = mine[:cut]
    ahead, behind = [[one, None]], [[one, None]]
    first = [send(one, 1), send(one, -1)]

    ids = (cand_owner * blocks + cand_local).reshape(per_home, seqs * NC)
    ids = [ids] + [send(ids, 0, d) for d in range(1, seqs)]
    me = jnp.stack([art // 2, art % 2, seq]).astype(jnp.int32)
    two = pack_stream(me, ids, mine, chips, blocks)
    second = [send(two, 1), send(two, -1)]
    ahead.append([first[0], second[0]])
    behind.append([first[1], second[1]])
    own = unit_blocks(lax.optimization_barrier((companies, *first))[0])
    other = lax.ppermute(companies, "art", [(i, i ^ 1) for i in range(arts)])
    other = unit_blocks(lax.optimization_barrier((other, *first))[0])

    def score(*pairs, others=()):
        return score_chunks(me, pairs, others, own, other, tokens, wide, deep, seqs)

    def after(array, *things):
        return lax.optimization_barrier((array, *things))[0]

    early = list(score((after(one, *second), two)))
    done = early[0]
    for d in range(1, half):
        a, b = [ahead[d][0], behind[d][0]], [ahead[d][1], behind[d][1]]
        if d == 1:
            b = [after(x, other) for x in b]
        else:
            fresh = after(ahead[d - 1][0], done, *a)
            more = score((fresh, ahead[d - 1][1]), behind[d - 1])
            early += more
            a = [after(x, done if d + 1 < half else more[0]) for x in a]
            b = [after(x, more[0]) for x in b]
            done = more[0]
        a, b = lax.optimization_barrier(a), lax.optimization_barrier(b)
        if d + 1 == half:
            ahead[d], behind[d] = [a[0], b[0]], [a[1], b[1]]
        if d + 1 < half:
            ahead.append([send(a[0], 1), send(b[0], 1)])
            behind.append([send(a[1], -1), send(b[1], -1)])
        else:
            last = (send(a[0], 1), send(b[1], -1))
    early += score(ahead[half - 1], behind[half - 1])
    spread = score(last, others=early)[1]
    parts = lax.all_to_all(spread, ("art", "seq"), split_axis=0, concat_axis=0, tiled=True)
    return tuple(close(parts.reshape(arts * seqs, -1, 128), articles, seqs))


def solution(mesh):
    chips = mesh.shape["art"] // 2
    wide = math.gcd(mesh.shape["seq"], chips)
    placed = (
        P("art", "seq", None, None),
        P(("art", "seq"), None, None),
        P(("art", "seq"), None, None),
        P("art", None, None),
    )
    return jax.shard_map(
        functools.partial(per_device, wide, chips // wide),
        mesh=mesh,
        in_specs=placed,
        out_specs=(P(("art", "seq"), None), P(("art", "seq"), None)),
        check_vma=False,
    )
```

```python
import functools
import math

import jax
import jax.numpy as jnp
from jax import lax
from jax.experimental import pallas as pl
from jax.experimental.pallas import tpu as pltpu
from jax.sharding import PartitionSpec as P

NC = 64
EPS = 1e-06
SHARP = 16.0
TEMPER = 4.0
GROUP = 4
UCOST = 4000000000
SCOST = 2.0
UNROLL = 20
PREP = 3
LAST = (((1,), (1,)), ((), ()))


def unit_kernel(parts, blocks_ref, out_ref, held_ref, sems):
    part = blocks_ref.shape[0] // parts
    copies = []
    for p in range(parts):
        rows = pl.ds(p * part, part)
        copies.append(pltpu.make_async_copy(blocks_ref.at[rows], held_ref.at[rows], sems.at[p]))
        copies[-1].start()
    for p in range(parts):
        copies[p].wait()

        def some(i, carry, p=p):
            rows = pl.ds(p * part + 2 * i, 2)
            wide = held_ref[rows].astype(jnp.float32)
            norm = jnp.sum(wide * wide, axis=-1, keepdims=True)
            out_ref[rows] = (wide * lax.rsqrt(norm + EPS)).astype(jnp.bfloat16)
            return carry

        lax.fori_loop(0, part // 2, some, 0, unroll=16)


def unit_blocks(blocks):
    parts = 4
    return pl.pallas_call(
        functools.partial(unit_kernel, parts),
        out_shape=jax.ShapeDtypeStruct(blocks.shape, jnp.bfloat16),
        in_specs=[pl.BlockSpec(memory_space=pltpu.HBM)],
        out_specs=pl.BlockSpec(memory_space=pltpu.VMEM),
        scratch_shapes=[
            pltpu.VMEM(blocks.shape, jnp.bfloat16),
            pltpu.SemaphoreType.DMA((parts,)),
        ],
        compiler_params=pltpu.CompilerParams(vmem_limit_bytes=32 * 1024 * 1024),
        cost_estimate=pl.CostEstimate(flops=UCOST, bytes_accessed=1, transcendentals=0),
        name="unit_blocks",
    )(blocks)


def mask(m):
    return m.astype(jnp.float32).astype(jnp.bfloat16)


def plan_rows(chips, articles):
    entries = -(-(articles * NC + chips * articles * (GROUP - 1)) // 128)
    return entries, -(-(3 * entries + 1) // 16) * 16


def pack_kernel(chips, blocks, me_ref, *refs):
    id_refs, query_ref, out_ref = refs[:-2], refs[-2], refs[-1]
    seqs = len(id_refs)
    core, seq = me_ref[1], me_ref[2]
    per_home, width = id_refs[0].shape
    rows = query_ref.shape[0]
    out_ref[0:rows, :] = query_ref[...]

    lane = lax.broadcasted_iota(jnp.int32, (per_home, width), 1)
    ids = jnp.zeros((per_home, width), jnp.int32)
    for d in range(seqs):
        table = id_refs[d][...]
        for p in range(seqs):
            k = (p + seqs - d) % seqs
            turned = table if k == p else pltpu.roll(table, (k - p) % seqs * NC, 1)
            ids = jnp.where((seq == p) & (lane // NC == k), turned, ids)
    ids = jnp.concatenate([ids[i : i + 1] for i in range(per_home)], axis=1)
    lanes = per_home * width
    articles = lanes // NC
    owner, local = ids // blocks, ids % blocks
    other = jnp.where(owner % 2 != core, 1, 0)
    here = owner // 2 == lax.broadcasted_iota(jnp.int32, (chips, lanes), 0)
    hot = mask(here)
    a = lax.broadcasted_iota(jnp.int32, (lanes, lanes), 0)
    b = lax.broadcasted_iota(jnp.int32, (lanes, lanes), 1)
    same = a // NC == b // NC
    rank = jnp.dot(hot, mask(same & (a <= b)), preferred_element_type=jnp.float32)
    amount = jnp.dot(hot, mask(same), preferred_element_type=jnp.float32).astype(jnp.int32)
    groups = (amount + (GROUP - 1)) // GROUP
    lead = lax.broadcasted_iota(jnp.int32, (chips, lanes), 1) % NC == 0
    tops = jnp.where(lead, groups, 0).astype(jnp.float32)
    ahead = jnp.dot(
        tops.astype(jnp.bfloat16), mask(a // NC < b // NC), preferred_element_type=jnp.float32
    )
    totals = jnp.sum(tops, axis=1, keepdims=True)
    lane = lax.broadcasted_iota(jnp.int32, (chips, 128), 1)
    before = lax.broadcasted_iota(jnp.int32, (chips, 128), 0) < lane % NC
    starts = jnp.sum(jnp.where(before, totals, 0.0), axis=0, keepdims=True).astype(jnp.int32)
    starts = jnp.where(lane[0:1] < NC, starts // 16, starts % 16).astype(jnp.float32)
    fence = mask(
        lax.broadcasted_iota(jnp.int32, (chips, chips), 1)
        < lax.broadcasted_iota(jnp.int32, (chips, chips), 0)
    )
    base = jnp.dot(fence, tops.astype(jnp.bfloat16), preferred_element_type=jnp.float32)
    base = jnp.sum(base, axis=1, keepdims=True)
    spot = jnp.where(here, GROUP * (base + ahead) + rank - 1.0, 0.0)
    spot = jnp.sum(spot, axis=0, keepdims=True).astype(jnp.int32)
    lane = lax.broadcasted_iota(jnp.int32, (1, lanes), 1)
    article = lane // NC % seqs * per_home + lane // width
    kinds = lax.broadcasted_iota(jnp.int32, (8, lanes), 0)
    fields = jnp.ones((8, lanes), jnp.int32)
    for k, row in enumerate((local, other * 128 + lane % NC, article)):
        fields = jnp.where(kinds == k, row, fields)
    entries, extra = plan_rows(chips, articles)
    slots = lax.broadcasted_iota(jnp.int32, (entries * 128, lanes), 0)
    got = lax.dot_general(
        fields.astype(jnp.float32).astype(jnp.bfloat16),
        mask(slots == spot),
        LAST,
        preferred_element_type=jnp.float32,
    )
    code = jnp.where(got[3:4] > 0.5, got[1:2], float(NC))
    lists = jnp.concatenate([got[0:1], code, got[2:3]], axis=1)
    lists = [lists[:, i * 128 : (i + 1) * 128] for i in range(3 * entries)]
    lists += [starts, jnp.zeros((extra - 3 * entries - 1, 128), jnp.float32)]
    out_ref[rows : rows + extra, :] = jnp.concatenate(lists, axis=0).astype(jnp.bfloat16)


def pack_stream(me, ids, query, chips, blocks):
    vmem = pl.BlockSpec(memory_space=pltpu.VMEM)
    articles = len(ids) * ids[0].shape[0]
    half = query.shape[0] // 2
    rows = half + plan_rows(chips, articles)[1]
    return pl.pallas_call(
        functools.partial(pack_kernel, chips, blocks),
        out_shape=jax.ShapeDtypeStruct((rows, query.shape[1]), jnp.bfloat16),
        grid=(1,),
        in_specs=[pl.BlockSpec(memory_space=pltpu.SMEM)]
        + [vmem] * len(ids)
        + [pl.BlockSpec((half, query.shape[1]), lambda i: (1, 0))],
        out_specs=vmem,
        compiler_params=pltpu.CompilerParams(vmem_limit_bytes=32 * 1024 * 1024),
        cost_estimate=pl.CostEstimate(flops=1, bytes_accessed=1, transcendentals=0),
        name="pack_stream",
    )(me, *ids, query)


def score_kernel(dims, me_ref, *refs):
    plans, others, seqs, blocks, wide, deep = dims
    chips = wide * deep
    pair_refs, refs = refs[: 2 * plans], refs[2 * plans :]
    other_refs, refs = refs[:others], refs[others:]
    own_ref, other_ref, *refs = refs
    out_refs = refs[:-6]
    turned_ref, scale_ref, mass_ref, words_ref, lists_ref, sems = refs[-6:]
    articles = turned_ref.shape[0] // plans
    tokens = mass_ref.shape[1]
    keys = own_ref.shape[1]
    half = mass_ref.shape[0] // plans
    entries, extra = plan_rows(chips, articles)
    bits = (2 * blocks - 1).bit_length()
    begin = articles // 2 * tokens

    copies = []
    for p in range(plans):
        rows = pair_refs[2 * p + 1][begin : begin + extra, :].astype(jnp.float32).astype(jnp.int32)
        local, code, article, starts = (rows[k * entries : (k + 1) * entries] for k in range(4))
        place = code % 128
        row = jnp.where(place < NC, article * NC + place, articles * NC)
        word = local + blocks * (code // 128) + 2 * blocks * row + (1 << 20) * article
        words_ref[p, 0:entries, :] = word
        words_ref[p, entries : entries + 1, :] = starts[0:1]
        copy = pltpu.make_async_copy(words_ref.at[p], lists_ref.at[p], sems.at[p])
        copy.start()
        copies.append(copy)

    def prepare(i, carry):
        for p, ref in enumerate(pair_refs):
            query = ref[pl.ds(pl.multiple_of(i * tokens, tokens), tokens), :]
            wide = query.astype(jnp.float32)
            norm = lax.dot_general(
                jnp.ones((8, query.shape[1]), jnp.bfloat16),
                (wide * wide).astype(jnp.bfloat16),
                LAST,
                preferred_element_type=jnp.float32,
            )
            at = p * (articles // 2) + i
            scale_ref[at] = lax.rsqrt(norm + EPS) * (SHARP * math.log2(math.e))
            turned_ref[at] = query.T
        return carry

    lax.fori_loop(0, articles // 2, prepare, 0, unroll=PREP)
    mass_ref[...] = jnp.ones_like(mass_ref)
    for copy in copies:
        copy.wait()

    chip = me_ref[0]
    begins = []
    counts = []
    for p in range(plans):
        low = lists_ref[p, entries, chip] * 16 + lists_ref[p, entries, NC + chip]
        high = lists_ref[p, entries, chip + 1] * 16 + lists_ref[p, entries, NC + chip + 1]
        begins.append(low)
        counts.append(high - low)
    total = sum(counts)

    def task(k):
        k = jnp.minimum(k, total - 1)
        if plans == 1:
            late, at = 0, (k + begins[0]) * GROUP
        else:
            late = (k >= counts[0]).astype(jnp.int32)
            at = (k + begins[0] + late * (begins[1] - begins[0] - counts[0])) * GROUP
        at = jnp.maximum(at, 0)
        line, spot = lax.shift_right_logical(at, 7), at & 127
        words = [lists_ref[late, line, spot + g] for g in range(GROUP)]
        article = lax.shift_right_logical(words[0], 20) + late * articles
        rows = [(lax.shift_right_logical(w, bits) & 2047) + late * half for w in words]
        return article, [w & (2 * blocks - 1) for w in words], rows

    def block(c):
        spot = c & (blocks - 1)
        return jnp.where(c >= blocks, other_ref[spot], own_ref[spot])

    def some(step, carry):
        for u in range(UNROLL):
            article, picks, rows = task(step * UNROLL + u)
            chosen = jnp.concatenate([block(c) for c in picks], axis=0)
            sims = jnp.dot(chosen, turned_ref[article], preferred_element_type=jnp.float32)
            grown = jnp.exp2(sims * scale_ref[article][0:1])
            for g, row in enumerate(rows):
                mass_ref[pl.ds(row, 1), :] = jnp.sum(
                    grown[g * keys : (g + 1) * keys], axis=0, keepdims=True
                )
        return carry

    lax.fori_loop(0, (total + UNROLL - 1) // UNROLL, some, 0)

    per_home = articles // seqs
    lane = lax.broadcasted_iota(jnp.int32, (NC, 128), 1)
    for p in range(plans):
        sums = jnp.zeros((NC, 128), jnp.float32)
        for i in range(articles):
            logs = jnp.log2(mass_ref[p * half + i * NC : p * half + (i + 1) * NC, :])
            sums = jnp.where(lane == i, jnp.sum(logs, axis=1, keepdims=True), sums)
        out_refs[p][:, 0:NC] = (sums * (math.log(2) / SHARP)).T[0:articles]
    if not others:
        return

    spread_ref = out_refs[-1]
    spread_ref[...] = jnp.zeros_like(spread_ref)
    block_rows = spread_ref.shape[0] // (2 * chips * seqs)
    side, rest = chip & (wide - 1), chip >> (wide.bit_length() - 1)
    place = side * deep + jnp.where(side & 1 == 0, rest, deep - 1 - rest)
    spots = [0] + [x for d in range(1, chips // 2) for x in (-d, d)] + [chips // 2]
    for spot, ref in zip(spots, [*other_refs, out_refs[0]]):
        at = (place + spot + chips) & (chips - 1)
        side, rest = at >> (deep.bit_length() - 1), at & (deep - 1)
        home = jnp.where(side & 1 == 0, rest, deep - 1 - rest) * wide + side
        for k in range(seqs):
            peer = (2 * home + me_ref[1]) * seqs + k
            rows = pl.ds(pl.multiple_of(peer * block_rows, 8), per_home)
            spread_ref[rows, :] = ref[k * per_home : (k + 1) * per_home, :]


def score_chunks(me, pairs, others, own, other, tokens, wide, deep, seqs):
    chips = wide * deep
    plans = len(pairs)
    blocks, keys, width = own.shape
    articles = 2 * pairs[0][0].shape[0] // tokens
    shapes = [jax.ShapeDtypeStruct((articles, 128), jnp.float32)] * plans
    if others:
        rows = -(-(articles // seqs) // 8) * 8 * 2 * chips * seqs
        shapes.append(jax.ShapeDtypeStruct((rows, 128), jnp.float32))
    lines = -(-(plan_rows(chips, articles)[0] + 1) // 8) * 8
    work = plans * articles * 8
    smem, vmem = pl.BlockSpec(memory_space=pltpu.SMEM), pl.BlockSpec(memory_space=pltpu.VMEM)
    return pl.pallas_call(
        functools.partial(score_kernel, (plans, len(others), seqs, blocks, wide, deep)),
        out_shape=shapes,
        in_specs=[smem] + [vmem] * (2 * plans + len(others) + 2),
        out_specs=[vmem] * len(shapes),
        scratch_shapes=[
            pltpu.VMEM((plans * articles, width, tokens), jnp.bfloat16),
            pltpu.VMEM((plans * articles, 8, tokens), jnp.float32),
            pltpu.VMEM((plans * (articles * NC + 8), tokens), jnp.float32),
            pltpu.VMEM((plans, lines, 128), jnp.int32),
            pltpu.SMEM((plans, lines, 128), jnp.int32),
            pltpu.SemaphoreType.DMA((plans,)),
        ],
        compiler_params=pltpu.CompilerParams(vmem_limit_bytes=32 * 1024 * 1024),
        cost_estimate=pl.CostEstimate(
            flops=int(SCOST * work * tokens * keys * width),
            bytes_accessed=4 * own.size,
            transcendentals=int(SCOST / 2 * work * tokens * keys),
        ),
        name="score_chunks",
    )(me, *[x for pair in pairs for x in pair], *others, own, other)


def close_kernel(seqs, parts_ref, relevance_ref, probs_ref, score_ref):
    peers = parts_ref.shape[0]
    rows = relevance_ref.shape[0] // seqs
    for d in range(seqs):
        part = parts_ref[d]
        for j in range(d + seqs, peers, seqs):
            part = part + parts_ref[j]
        for i in range(rows):
            score_ref[i * seqs + d : i * seqs + d + 1, :] = part[i : i + 1]
    score = score_ref[:, 0:NC]
    relevance = score - jnp.mean(score, axis=-1, keepdims=True)
    weights = jnp.exp(TEMPER * relevance)
    relevance_ref[...] = relevance
    probs_ref[...] = weights / jnp.sum(weights, axis=-1, keepdims=True)


def close(parts, articles, seqs):
    vmem = pl.BlockSpec(memory_space=pltpu.VMEM)
    return pl.pallas_call(
        functools.partial(close_kernel, seqs),
        out_shape=[jax.ShapeDtypeStruct((articles, NC), jnp.float32)] * 2,
        in_specs=[vmem],
        out_specs=[vmem] * 2,
        scratch_shapes=[pltpu.VMEM((articles, 128), jnp.float32)],
        name="close",
    )(parts)


def per_device(wide, deep, queries, cand_owner, cand_local, companies):
    articles = queries.shape[0]
    seqs, arts = lax.axis_size("seq"), lax.axis_size("art")
    art, seq = lax.axis_index("art"), lax.axis_index("seq")
    chips = wide * deep
    half = chips // 2
    per_home = articles // seqs
    blocks = companies.shape[0]
    tokens = queries.shape[2]
    mine = queries.reshape(articles * tokens, queries.shape[3])
    ring = []
    for y in range(wide):
        for z in range(deep) if y % 2 == 0 else reversed(range(deep)):
            ring.append(z * wide + y)

    def turn(step, across=0):
        return [
            (
                (2 * ring[i] + c) * seqs + s,
                (2 * ring[(i + step) % chips] + c) * seqs + (s + across) % seqs,
            )
            for i in range(chips)
            for c in range(2)
            for s in range(seqs)
        ]

    def send(array, step, across=0):
        return lax.ppermute(array, ("art", "seq"), turn(step, across))

    cut = articles // 2 * tokens
    one = mine[:cut]
    ahead, behind = [[one, None]], [[one, None]]
    first = [send(one, 1), send(one, -1)]

    ids = (cand_owner * blocks + cand_local).reshape(per_home, seqs * NC)
    ids = [ids] + [send(ids, 0, d) for d in range(1, seqs)]
    me = jnp.stack([art // 2, art % 2, seq]).astype(jnp.int32)
    two = pack_stream(me, ids, mine, chips, blocks)
    second = [send(two, 1), send(two, -1)]
    ahead.append([first[0], second[0]])
    behind.append([first[1], second[1]])
    own = unit_blocks(lax.optimization_barrier((companies, *first))[0])
    other = lax.ppermute(companies, "art", [(i, i ^ 1) for i in range(arts)])
    other = unit_blocks(lax.optimization_barrier((other, *first))[0])

    def score(*pairs, others=()):
        return score_chunks(me, pairs, others, own, other, tokens, wide, deep, seqs)

    def after(array, *things):
        return lax.optimization_barrier((array, *things))[0]

    early = list(score((after(one, *second), two)))
    done = early[0]
    for d in range(1, half):
        a, b = [ahead[d][0], behind[d][0]], [ahead[d][1], behind[d][1]]
        if d == 1:
            b = [after(x, other) for x in b]
        else:
            fresh = after(ahead[d - 1][0], done, *a)
            more = score((fresh, ahead[d - 1][1]), behind[d - 1])
            early += more
            a = [after(x, done if d + 1 < half else more[0]) for x in a]
            b = [after(x, more[0]) for x in b]
            done = more[0]
        a, b = lax.optimization_barrier(a), lax.optimization_barrier(b)
        if d + 1 == half:
            ahead[d], behind[d] = [a[0], b[0]], [a[1], b[1]]
        if d + 1 < half:
            ahead.append([send(a[0], 1), send(b[0], 1)])
            behind.append([send(a[1], -1), send(b[1], -1)])
        else:
            last = (send(a[0], 1), send(b[1], -1))
    early += score(ahead[half - 1], behind[half - 1])
    spread = score(last, others=early)[1]
    parts = lax.all_to_all(spread, ("art", "seq"), split_axis=0, concat_axis=0, tiled=True)
    return tuple(close(parts.reshape(arts * seqs, -1, 128), articles, seqs))


def solution(mesh):
    chips = mesh.shape["art"] // 2
    wide = math.gcd(mesh.shape["seq"], chips)
    placed = (
        P("art", "seq", None, None),
        P(("art", "seq"), None, None),
        P(("art", "seq"), None, None),
        P("art", None, None),
    )
    return jax.shard_map(
        functools.partial(per_device, wide, chips // wide),
        mesh=mesh,
        in_specs=placed,
        out_specs=(P(("art", "seq"), None), P(("art", "seq"), None)),
        check_vma=False,
    )
```

```python
import functools
import math

import jax
import jax.numpy as jnp
from jax import lax
from jax.experimental import pallas as pl
from jax.experimental.pallas import tpu as pltpu
from jax.sharding import PartitionSpec as P

NC = 64
EPS = 1e-06
SHARP = 16.0
TEMPER = 4.0
GROUP = 4
UCOST = 4000000000
SCOST = 2.0
UNROLL = 20
PREP = 3
LAST = (((1,), (1,)), ((), ()))


def unit_kernel(parts, blocks_ref, out_ref, held_ref, sems):
    part = blocks_ref.shape[0] // parts
    copies = []
    for p in range(parts):
        rows = pl.ds(p * part, part)
        copies.append(pltpu.make_async_copy(blocks_ref.at[rows], held_ref.at[rows], sems.at[p]))
        copies[-1].start()
    for p in range(parts):
        copies[p].wait()

        def some(i, carry, p=p):
            rows = pl.ds(p * part + 2 * i, 2)
            wide = held_ref[rows].astype(jnp.float32)
            norm = jnp.sum(wide * wide, axis=-1, keepdims=True)
            out_ref[rows] = (wide * lax.rsqrt(norm + EPS)).astype(jnp.bfloat16)
            return carry

        lax.fori_loop(0, part // 2, some, 0, unroll=16)


def unit_blocks(blocks):
    parts = 4
    return pl.pallas_call(
        functools.partial(unit_kernel, parts),
        out_shape=jax.ShapeDtypeStruct(blocks.shape, jnp.bfloat16),
        in_specs=[pl.BlockSpec(memory_space=pltpu.HBM)],
        out_specs=pl.BlockSpec(memory_space=pltpu.VMEM),
        scratch_shapes=[
            pltpu.VMEM(blocks.shape, jnp.bfloat16),
            pltpu.SemaphoreType.DMA((parts,)),
        ],
        compiler_params=pltpu.CompilerParams(vmem_limit_bytes=32 * 1024 * 1024),
        cost_estimate=pl.CostEstimate(flops=UCOST, bytes_accessed=1, transcendentals=0),
        name="unit_blocks",
    )(blocks)


def mask(m):
    return m.astype(jnp.float32).astype(jnp.bfloat16)


def plan_rows(chips, articles):
    entries = -(-(articles * NC + chips * articles * (GROUP - 1)) // 128)
    return entries, -(-(3 * entries + 1) // 16) * 16


def pack_kernel(chips, blocks, me_ref, *refs):
    id_refs, (query_ref, ahead_ref, behind_ref, lists_ref) = refs[:-4], refs[-4:]
    seqs = len(id_refs)
    core, seq = me_ref[1], me_ref[2]
    per_home, width = id_refs[0].shape
    rows = query_ref.shape[0] // 2
    ahead_ref[0:rows, :] = query_ref[rows : 2 * rows, :]
    behind_ref[0:rows, :] = query_ref[0:rows, :]

    lane = lax.broadcasted_iota(jnp.int32, (per_home, width), 1)
    ids = jnp.zeros((per_home, width), jnp.int32)
    for d in range(seqs):
        table = id_refs[d][...]
        for p in range(seqs):
            k = (p + seqs - d) % seqs
            turned = table if k == p else pltpu.roll(table, (k - p) % seqs * NC, 1)
            ids = jnp.where((seq == p) & (lane // NC == k), turned, ids)
    ids = jnp.concatenate([ids[i : i + 1] for i in range(per_home)], axis=1)
    lanes = per_home * width
    articles = lanes // NC
    owner, local = ids // blocks, ids % blocks
    other = jnp.where(owner % 2 != core, 1, 0)
    here = owner // 2 == lax.broadcasted_iota(jnp.int32, (chips, lanes), 0)
    hot = mask(here)
    a = lax.broadcasted_iota(jnp.int32, (lanes, lanes), 0)
    b = lax.broadcasted_iota(jnp.int32, (lanes, lanes), 1)
    same = a // NC == b // NC
    rank = jnp.dot(hot, mask(same & (a <= b)), preferred_element_type=jnp.float32)
    amount = jnp.dot(hot, mask(same), preferred_element_type=jnp.float32).astype(jnp.int32)
    groups = (amount + (GROUP - 1)) // GROUP
    lead = lax.broadcasted_iota(jnp.int32, (chips, lanes), 1) % NC == 0
    tops = jnp.where(lead, groups, 0).astype(jnp.float32)
    ahead = jnp.dot(
        tops.astype(jnp.bfloat16), mask(a // NC < b // NC), preferred_element_type=jnp.float32
    )
    totals = jnp.sum(tops, axis=1, keepdims=True)
    lane = lax.broadcasted_iota(jnp.int32, (chips, 128), 1)
    before = lax.broadcasted_iota(jnp.int32, (chips, 128), 0) < lane % NC
    starts = jnp.sum(jnp.where(before, totals, 0.0), axis=0, keepdims=True).astype(jnp.int32)
    starts = jnp.where(lane[0:1] < NC, starts // 16, starts % 16).astype(jnp.float32)
    fence = mask(
        lax.broadcasted_iota(jnp.int32, (chips, chips), 1)
        < lax.broadcasted_iota(jnp.int32, (chips, chips), 0)
    )
    base = jnp.dot(fence, tops.astype(jnp.bfloat16), preferred_element_type=jnp.float32)
    base = jnp.sum(base, axis=1, keepdims=True)
    spot = jnp.where(here, GROUP * (base + ahead) + rank - 1.0, 0.0)
    spot = jnp.sum(spot, axis=0, keepdims=True).astype(jnp.int32)
    lane = lax.broadcasted_iota(jnp.int32, (1, lanes), 1)
    article = lane // NC % seqs * per_home + lane // width
    kinds = lax.broadcasted_iota(jnp.int32, (8, lanes), 0)
    fields = jnp.ones((8, lanes), jnp.int32)
    for k, row in enumerate((local, other * 128 + lane % NC, article)):
        fields = jnp.where(kinds == k, row, fields)
    entries, extra = plan_rows(chips, articles)
    slots = lax.broadcasted_iota(jnp.int32, (entries * 128, lanes), 0)
    got = lax.dot_general(
        fields.astype(jnp.float32).astype(jnp.bfloat16),
        mask(slots == spot),
        LAST,
        preferred_element_type=jnp.float32,
    )
    code = jnp.where(got[3:4] > 0.5, got[1:2], float(NC))
    lists = jnp.concatenate([got[0:1], code, got[2:3]], axis=1)
    lists = [lists[:, i * 128 : (i + 1) * 128] for i in range(3 * entries)]
    lists += [starts, jnp.zeros((extra - 3 * entries - 1, 128), jnp.float32)]
    lists = jnp.concatenate(lists, axis=0).astype(jnp.bfloat16)
    ahead_ref[rows : rows + extra, :] = lists
    behind_ref[rows : rows + extra, :] = lists
    lists_ref[...] = lists


def pack_streams(me, ids, query, chips, blocks):
    vmem = pl.BlockSpec(memory_space=pltpu.VMEM)
    articles = len(ids) * ids[0].shape[0]
    extra = plan_rows(chips, articles)[1]
    shapes = [(query.shape[0] // 2 + extra, query.shape[1])] * 2 + [(extra, query.shape[1])]
    return pl.pallas_call(
        functools.partial(pack_kernel, chips, blocks),
        out_shape=[jax.ShapeDtypeStruct(shape, jnp.bfloat16) for shape in shapes],
        in_specs=[pl.BlockSpec(memory_space=pltpu.SMEM)] + [vmem] * (len(ids) + 1),
        out_specs=[vmem] * 3,
        compiler_params=pltpu.CompilerParams(vmem_limit_bytes=32 * 1024 * 1024),
        cost_estimate=pl.CostEstimate(flops=1, bytes_accessed=1, transcendentals=0),
        name="pack_streams",
    )(me, *ids, query)


def score_kernel(dims, me_ref, *refs):
    plans, apart, others, seqs, blocks, wide, deep = dims
    chips = wide * deep
    pair_refs, refs = refs[: 2 * plans], refs[2 * plans :]
    far_refs, refs = refs[:apart], refs[apart:]
    other_refs, refs = refs[:others], refs[others:]
    own_ref, other_ref, *refs = refs
    out_refs = refs[:-6]
    turned_ref, scale_ref, mass_ref, words_ref, lists_ref, sems = refs[-6:]
    articles = turned_ref.shape[0] // plans
    tokens = mass_ref.shape[1]
    keys = own_ref.shape[1]
    half = mass_ref.shape[0] // plans
    entries, extra = plan_rows(chips, articles)
    bits = (2 * blocks - 1).bit_length()
    begin = articles // 2 * tokens

    copies = []
    for p in range(plans):
        rows = far_refs[0][...] if apart else pair_refs[2 * p + 1][begin : begin + extra, :]
        rows = rows.astype(jnp.float32).astype(jnp.int32)
        local, code, article, starts = (rows[k * entries : (k + 1) * entries] for k in range(4))
        place = code % 128
        row = jnp.where(place < NC, article * NC + place, articles * NC)
        word = local + blocks * (code // 128) + 2 * blocks * row + (1 << 20) * article
        words_ref[p, 0:entries, :] = word
        words_ref[p, entries : entries + 1, :] = starts[0:1]
        copy = pltpu.make_async_copy(words_ref.at[p], lists_ref.at[p], sems.at[p])
        copy.start()
        copies.append(copy)

    def prepare(i, carry):
        for p, ref in enumerate(pair_refs):
            query = ref[pl.ds(pl.multiple_of(i * tokens, tokens), tokens), :]
            wide = query.astype(jnp.float32)
            norm = lax.dot_general(
                jnp.ones((8, query.shape[1]), jnp.bfloat16),
                (wide * wide).astype(jnp.bfloat16),
                LAST,
                preferred_element_type=jnp.float32,
            )
            late = p % 2 if p < 2 else 1 - p % 2
            at = p // 2 * articles + late * (articles // 2) + i
            scale_ref[at] = lax.rsqrt(norm + EPS) * (SHARP * math.log2(math.e))
            turned_ref[at] = query.T
        return carry

    lax.fori_loop(0, articles // 2, prepare, 0, unroll=PREP)
    mass_ref[...] = jnp.ones_like(mass_ref)
    for copy in copies:
        copy.wait()

    chip = me_ref[0]
    begins = []
    counts = []
    for p in range(plans):
        low = lists_ref[p, entries, chip] * 16 + lists_ref[p, entries, NC + chip]
        high = lists_ref[p, entries, chip + 1] * 16 + lists_ref[p, entries, NC + chip + 1]
        begins.append(low)
        counts.append(high - low)
    total = sum(counts)

    def task(k):
        k = jnp.minimum(k, total - 1)
        if plans == 1:
            late, at = 0, (k + begins[0]) * GROUP
        else:
            late = (k >= counts[0]).astype(jnp.int32)
            at = (k + begins[0] + late * (begins[1] - begins[0] - counts[0])) * GROUP
        at = jnp.maximum(at, 0)
        line, spot = lax.shift_right_logical(at, 7), at & 127
        words = [lists_ref[late, line, spot + g] for g in range(GROUP)]
        article = lax.shift_right_logical(words[0], 20) + late * articles
        rows = [(lax.shift_right_logical(w, bits) & 2047) + late * half for w in words]
        return article, [w & (2 * blocks - 1) for w in words], rows

    def block(c):
        spot = c & (blocks - 1)
        return jnp.where(c >= blocks, other_ref[spot], own_ref[spot])

    def some(step, carry):
        for u in range(UNROLL):
            article, picks, rows = task(step * UNROLL + u)
            chosen = jnp.concatenate([block(c) for c in picks], axis=0)
            sims = jnp.dot(chosen, turned_ref[article], preferred_element_type=jnp.float32)
            grown = jnp.exp2(sims * scale_ref[article][0:1])
            for g, row in enumerate(rows):
                mass_ref[pl.ds(row, 1), :] = jnp.sum(
                    grown[g * keys : (g + 1) * keys], axis=0, keepdims=True
                )
        return carry

    lax.fori_loop(0, (total + UNROLL - 1) // UNROLL, some, 0)

    per_home = articles // seqs
    lane = lax.broadcasted_iota(jnp.int32, (NC, 128), 1)
    for p in range(plans):
        sums = jnp.zeros((NC, 128), jnp.float32)
        for i in range(articles):
            logs = jnp.log2(mass_ref[p * half + i * NC : p * half + (i + 1) * NC, :])
            sums = jnp.where(lane == i, jnp.sum(logs, axis=1, keepdims=True), sums)
        out_refs[p][:, 0:NC] = (sums * (math.log(2) / SHARP)).T[0:articles]
    if not others:
        return

    spread_ref = out_refs[-1]
    spread_ref[...] = jnp.zeros_like(spread_ref)
    block_rows = spread_ref.shape[0] // (2 * chips * seqs)
    side, rest = chip & (wide - 1), chip >> (wide.bit_length() - 1)
    place = side * deep + jnp.where(side & 1 == 0, rest, deep - 1 - rest)
    spots = [0] + [x for d in range(1, chips // 2) for x in (-d, d)] + [chips // 2]
    for spot, ref in zip(spots, [*other_refs, out_refs[0]]):
        at = (place + spot + chips) & (chips - 1)
        side, rest = at >> (deep.bit_length() - 1), at & (deep - 1)
        home = jnp.where(side & 1 == 0, rest, deep - 1 - rest) * wide + side
        for k in range(seqs):
            peer = (2 * home + me_ref[1]) * seqs + k
            rows = pl.ds(pl.multiple_of(peer * block_rows, 8), per_home)
            spread_ref[rows, :] = ref[k * per_home : (k + 1) * per_home, :]


def score_chunks(me, pairs, far, others, own, other, tokens, wide, deep, seqs):
    chips = wide * deep
    plans = len(pairs)
    blocks, keys, width = own.shape
    articles = 2 * pairs[0][0].shape[0] // tokens
    shapes = [jax.ShapeDtypeStruct((articles, 128), jnp.float32)] * plans
    if others:
        rows = -(-(articles // seqs) // 8) * 8 * 2 * chips * seqs
        shapes.append(jax.ShapeDtypeStruct((rows, 128), jnp.float32))
    lines = -(-(plan_rows(chips, articles)[0] + 1) // 8) * 8
    work = plans * articles * 8
    smem, vmem = pl.BlockSpec(memory_space=pltpu.SMEM), pl.BlockSpec(memory_space=pltpu.VMEM)
    return pl.pallas_call(
        functools.partial(score_kernel, (plans, len(far), len(others), seqs, blocks, wide, deep)),
        out_shape=shapes,
        in_specs=[smem] + [vmem] * (2 * plans + len(far) + len(others) + 2),
        out_specs=[vmem] * len(shapes),
        scratch_shapes=[
            pltpu.VMEM((plans * articles, width, tokens), jnp.bfloat16),
            pltpu.VMEM((plans * articles, 8, tokens), jnp.float32),
            pltpu.VMEM((plans * (articles * NC + 8), tokens), jnp.float32),
            pltpu.VMEM((plans, lines, 128), jnp.int32),
            pltpu.SMEM((plans, lines, 128), jnp.int32),
            pltpu.SemaphoreType.DMA((plans,)),
        ],
        compiler_params=pltpu.CompilerParams(vmem_limit_bytes=32 * 1024 * 1024),
        cost_estimate=pl.CostEstimate(
            flops=int(SCOST * work * tokens * keys * width),
            bytes_accessed=4 * own.size,
            transcendentals=int(SCOST / 2 * work * tokens * keys),
        ),
        name="score_chunks",
    )(me, *[x for pair in pairs for x in pair], *far, *others, own, other)


def close_kernel(seqs, parts_ref, relevance_ref, probs_ref, score_ref):
    peers = parts_ref.shape[0]
    rows = relevance_ref.shape[0] // seqs
    for d in range(seqs):
        part = parts_ref[d]
        for j in range(d + seqs, peers, seqs):
            part = part + parts_ref[j]
        for i in range(rows):
            score_ref[i * seqs + d : i * seqs + d + 1, :] = part[i : i + 1]
    score = score_ref[:, 0:NC]
    relevance = score - jnp.mean(score, axis=-1, keepdims=True)
    weights = jnp.exp(TEMPER * relevance)
    relevance_ref[...] = relevance
    probs_ref[...] = weights / jnp.sum(weights, axis=-1, keepdims=True)


def close(parts, articles, seqs):
    vmem = pl.BlockSpec(memory_space=pltpu.VMEM)
    return pl.pallas_call(
        functools.partial(close_kernel, seqs),
        out_shape=[jax.ShapeDtypeStruct((articles, NC), jnp.float32)] * 2,
        in_specs=[vmem],
        out_specs=[vmem] * 2,
        scratch_shapes=[pltpu.VMEM((articles, 128), jnp.float32)],
        name="close",
    )(parts)


def per_device(wide, deep, queries, cand_owner, cand_local, companies):
    articles = queries.shape[0]
    seqs, arts = lax.axis_size("seq"), lax.axis_size("art")
    art, seq = lax.axis_index("art"), lax.axis_index("seq")
    chips = wide * deep
    half = chips // 2
    per_home = articles // seqs
    blocks = companies.shape[0]
    tokens = queries.shape[2]
    mine = queries.reshape(articles * tokens, queries.shape[3])
    ring = []
    for y in range(wide):
        for z in range(deep) if y % 2 == 0 else reversed(range(deep)):
            ring.append(z * wide + y)

    def turn(step, across=0):
        return [
            (
                (2 * ring[i] + c) * seqs + s,
                (2 * ring[(i + step) % chips] + c) * seqs + (s + across) % seqs,
            )
            for i in range(chips)
            for c in range(2)
            for s in range(seqs)
        ]

    def send(array, step, across=0):
        return lax.ppermute(array, ("art", "seq"), turn(step, across))

    cut = articles // 2 * tokens
    one = mine[:cut]
    ahead, behind = [None], [None]
    first = [send(one, 1), send(mine[cut:], -1)]

    ids = (cand_owner * blocks + cand_local).reshape(per_home, seqs * NC)
    ids = [ids] + [send(ids, 0, d) for d in range(1, seqs)]
    me = jnp.stack([art // 2, art % 2, seq]).astype(jnp.int32)
    two, back, lists = pack_streams(me, ids, mine, chips, blocks)
    second = [send(two, 1), send(back, -1)]
    ahead.append([first[0], second[0]])
    behind.append([first[1], second[1]])
    own = unit_blocks(lax.optimization_barrier((companies, *first))[0])
    other = lax.ppermute(companies, "art", [(i, i ^ 1) for i in range(arts)])
    other = unit_blocks(lax.optimization_barrier((other, *first))[0])

    def score(*pairs, far=(), others=()):
        return score_chunks(me, pairs, far, others, own, other, tokens, wide, deep, seqs)

    def after(array, *things):
        return lax.optimization_barrier((array, *things))[0]

    early = list(score((after(one, *second), two)))
    done = early[0]
    far = send(after(lists, done), half)
    for d in range(1, half):
        a, b = [ahead[d][0], behind[d][0]], [ahead[d][1], behind[d][1]]
        if d == 1:
            b = [after(x, own) for x in b]
        else:
            fresh = after(ahead[d - 1][0], done, *a, *([far] if d == 3 else []))
            more = score((fresh, ahead[d - 1][1]), behind[d - 1])
            early += more
            a = [after(x, done if d + 1 < half else more[0]) for x in a]
            b = [after(x, more[0]) for x in b]
            done = more[0]
        a, b = lax.optimization_barrier(a), lax.optimization_barrier(b)
        if d + 1 < half:
            ahead.append([send(a[0], 1), send(b[0], 1)])
            behind.append([send(a[1], -1), send(b[1], -1)])
        else:
            ahead[d][0] = a[0]
            last = (send(a[0], 1), send(a[1], -1))
    early += score(ahead[half - 1], behind[half - 1])
    spread = score(last, far=(far,), others=early)[1]
    parts = lax.all_to_all(spread, ("art", "seq"), split_axis=0, concat_axis=0, tiled=True)
    return tuple(close(parts.reshape(arts * seqs, -1, 128), articles, seqs))


def solution(mesh):
    chips = mesh.shape["art"] // 2
    wide = math.gcd(mesh.shape["seq"], chips)
    placed = (
        P("art", "seq", None, None),
        P(("art", "seq"), None, None),
        P(("art", "seq"), None, None),
        P("art", None, None),
    )
    return jax.shard_map(
        functools.partial(per_device, wide, chips // wide),
        mesh=mesh,
        in_specs=placed,
        out_specs=(P(("art", "seq"), None), P(("art", "seq"), None)),
        check_vma=False,
    )
```

```python
import functools
import math

import jax
import jax.numpy as jnp
from jax import lax
from jax.experimental import pallas as pl
from jax.experimental.pallas import tpu as pltpu
from jax.sharding import PartitionSpec as P

NC = 64
EPS = 1e-06
SHARP = 16.0
TEMPER = 4.0
GROUP = 4
UCOST = 4000000000
SCOST = 2.0
UNROLL = 20
PREP = 3
LAST = (((1,), (1,)), ((), ()))


def unit_kernel(parts, blocks_ref, out_ref, held_ref, sems):
    part = blocks_ref.shape[0] // parts
    copies = []
    for p in range(parts):
        rows = pl.ds(p * part, part)
        copies.append(pltpu.make_async_copy(blocks_ref.at[rows], held_ref.at[rows], sems.at[p]))
        copies[-1].start()
    for p in range(parts):
        copies[p].wait()

        def some(i, carry, p=p):
            rows = pl.ds(p * part + 2 * i, 2)
            wide = held_ref[rows].astype(jnp.float32)
            norm = jnp.sum(wide * wide, axis=-1, keepdims=True)
            out_ref[rows] = (wide * lax.rsqrt(norm + EPS)).astype(jnp.bfloat16)
            return carry

        lax.fori_loop(0, part // 2, some, 0, unroll=16)


def unit_blocks(blocks):
    parts = 4
    return pl.pallas_call(
        functools.partial(unit_kernel, parts),
        out_shape=jax.ShapeDtypeStruct(blocks.shape, jnp.bfloat16),
        in_specs=[pl.BlockSpec(memory_space=pltpu.HBM)],
        out_specs=pl.BlockSpec(memory_space=pltpu.VMEM),
        scratch_shapes=[
            pltpu.VMEM(blocks.shape, jnp.bfloat16),
            pltpu.SemaphoreType.DMA((parts,)),
        ],
        compiler_params=pltpu.CompilerParams(vmem_limit_bytes=32 * 1024 * 1024),
        cost_estimate=pl.CostEstimate(flops=UCOST, bytes_accessed=1, transcendentals=0),
        name="unit_blocks",
    )(blocks)


def mask(m):
    return m.astype(jnp.float32).astype(jnp.bfloat16)


def plan_rows(chips, articles):
    entries = -(-(articles * NC + chips * articles * (GROUP - 1)) // 128)
    return entries, -(-(3 * entries + 1) // 16) * 16


def pack_kernel(chips, blocks, me_ref, *refs):
    id_refs, (first_ref, second_ref, ahead_ref, behind_ref, lists_ref) = refs[:-5], refs[-5:]
    seqs = len(id_refs)
    core, seq = me_ref[1], me_ref[2]
    per_home, width = id_refs[0].shape
    rows = first_ref.shape[0]
    ahead_ref[0:rows, :] = second_ref[...]
    behind_ref[0:rows, :] = first_ref[...]

    lane = lax.broadcasted_iota(jnp.int32, (per_home, width), 1)
    ids = jnp.zeros((per_home, width), jnp.int32)
    for d in range(seqs):
        table = id_refs[d][...]
        for p in range(seqs):
            k = (p + seqs - d) % seqs
            turned = table if k == p else pltpu.roll(table, (k - p) % seqs * NC, 1)
            ids = jnp.where((seq == p) & (lane // NC == k), turned, ids)
    ids = jnp.concatenate([ids[i : i + 1] for i in range(per_home)], axis=1)
    lanes = per_home * width
    articles = lanes // NC
    owner, local = ids // blocks, ids % blocks
    other = jnp.where(owner % 2 != core, 1, 0)
    here = owner // 2 == lax.broadcasted_iota(jnp.int32, (chips, lanes), 0)
    hot = mask(here)
    a = lax.broadcasted_iota(jnp.int32, (lanes, lanes), 0)
    b = lax.broadcasted_iota(jnp.int32, (lanes, lanes), 1)
    same = a // NC == b // NC
    rank = jnp.dot(hot, mask(same & (a <= b)), preferred_element_type=jnp.float32)
    amount = jnp.dot(hot, mask(same), preferred_element_type=jnp.float32).astype(jnp.int32)
    groups = (amount + (GROUP - 1)) // GROUP
    lead = lax.broadcasted_iota(jnp.int32, (chips, lanes), 1) % NC == 0
    tops = jnp.where(lead, groups, 0).astype(jnp.float32)
    ahead = jnp.dot(
        tops.astype(jnp.bfloat16), mask(a // NC < b // NC), preferred_element_type=jnp.float32
    )
    totals = jnp.sum(tops, axis=1, keepdims=True)
    lane = lax.broadcasted_iota(jnp.int32, (chips, 128), 1)
    before = lax.broadcasted_iota(jnp.int32, (chips, 128), 0) < lane % NC
    starts = jnp.sum(jnp.where(before, totals, 0.0), axis=0, keepdims=True).astype(jnp.int32)
    starts = jnp.where(lane[0:1] < NC, starts // 16, starts % 16).astype(jnp.float32)
    fence = mask(
        lax.broadcasted_iota(jnp.int32, (chips, chips), 1)
        < lax.broadcasted_iota(jnp.int32, (chips, chips), 0)
    )
    base = jnp.dot(fence, tops.astype(jnp.bfloat16), preferred_element_type=jnp.float32)
    base = jnp.sum(base, axis=1, keepdims=True)
    spot = jnp.where(here, GROUP * (base + ahead) + rank - 1.0, 0.0)
    spot = jnp.sum(spot, axis=0, keepdims=True).astype(jnp.int32)
    lane = lax.broadcasted_iota(jnp.int32, (1, lanes), 1)
    article = lane // NC % seqs * per_home + lane // width
    kinds = lax.broadcasted_iota(jnp.int32, (8, lanes), 0)
    fields = jnp.ones((8, lanes), jnp.int32)
    for k, row in enumerate((local, other * 128 + lane % NC, article)):
        fields = jnp.where(kinds == k, row, fields)
    entries, extra = plan_rows(chips, articles)
    slots = lax.broadcasted_iota(jnp.int32, (entries * 128, lanes), 0)
    got = lax.dot_general(
        fields.astype(jnp.float32).astype(jnp.bfloat16),
        mask(slots == spot),
        LAST,
        preferred_element_type=jnp.float32,
    )
    code = jnp.where(got[3:4] > 0.5, got[1:2], float(NC))
    lists = jnp.concatenate([got[0:1], code, got[2:3]], axis=1)
    lists = [lists[:, i * 128 : (i + 1) * 128] for i in range(3 * entries)]
    lists += [starts, jnp.zeros((extra - 3 * entries - 1, 128), jnp.float32)]
    lists = jnp.concatenate(lists, axis=0).astype(jnp.bfloat16)
    ahead_ref[rows : rows + extra, :] = lists
    behind_ref[rows : rows + extra, :] = lists
    lists_ref[...] = lists


def pack_streams(me, ids, first, second, chips, blocks):
    vmem = pl.BlockSpec(memory_space=pltpu.VMEM)
    articles = len(ids) * ids[0].shape[0]
    extra = plan_rows(chips, articles)[1]
    shapes = [(first.shape[0] + extra, first.shape[1])] * 2 + [(extra, first.shape[1])]
    return pl.pallas_call(
        functools.partial(pack_kernel, chips, blocks),
        out_shape=[jax.ShapeDtypeStruct(shape, jnp.bfloat16) for shape in shapes],
        in_specs=[pl.BlockSpec(memory_space=pltpu.SMEM)] + [vmem] * (len(ids) + 2),
        out_specs=[vmem] * 3,
        compiler_params=pltpu.CompilerParams(vmem_limit_bytes=32 * 1024 * 1024),
        cost_estimate=pl.CostEstimate(flops=1, bytes_accessed=1, transcendentals=0),
        name="pack_streams",
    )(me, *ids, first, second)


def score_kernel(dims, me_ref, *refs):
    plans, apart, others, seqs, blocks, wide, deep = dims
    chips = wide * deep
    pair_refs, refs = refs[: 2 * plans], refs[2 * plans :]
    far_refs, refs = refs[:apart], refs[apart:]
    other_refs, refs = refs[:others], refs[others:]
    own_ref, other_ref, *refs = refs
    out_refs = refs[:-6]
    turned_ref, scale_ref, mass_ref, words_ref, lists_ref, sems = refs[-6:]
    articles = turned_ref.shape[0] // plans
    tokens = mass_ref.shape[1]
    keys = own_ref.shape[1]
    half = mass_ref.shape[0] // plans
    entries, extra = plan_rows(chips, articles)
    bits = (2 * blocks - 1).bit_length()
    begin = articles // 2 * tokens

    copies = []
    for p in range(plans):
        rows = far_refs[0][...] if apart else pair_refs[2 * p + 1][begin : begin + extra, :]
        rows = rows.astype(jnp.float32).astype(jnp.int32)
        local, code, article, starts = (rows[k * entries : (k + 1) * entries] for k in range(4))
        place = code % 128
        row = jnp.where(place < NC, article * NC + place, articles * NC)
        word = local + blocks * (code // 128) + 2 * blocks * row + (1 << 20) * article
        words_ref[p, 0:entries, :] = word
        words_ref[p, entries : entries + 1, :] = starts[0:1]
        copy = pltpu.make_async_copy(words_ref.at[p], lists_ref.at[p], sems.at[p])
        copy.start()
        copies.append(copy)

    def prepare(i, carry):
        for p, ref in enumerate(pair_refs):
            query = ref[pl.ds(pl.multiple_of(i * tokens, tokens), tokens), :]
            wide = query.astype(jnp.float32)
            norm = lax.dot_general(
                jnp.ones((8, query.shape[1]), jnp.bfloat16),
                (wide * wide).astype(jnp.bfloat16),
                LAST,
                preferred_element_type=jnp.float32,
            )
            late = p % 2 if p < 2 else 1 - p % 2
            at = p // 2 * articles + late * (articles // 2) + i
            scale_ref[at] = lax.rsqrt(norm + EPS) * (SHARP * math.log2(math.e))
            turned_ref[at] = query.T
        return carry

    lax.fori_loop(0, articles // 2, prepare, 0, unroll=PREP)
    mass_ref[...] = jnp.ones_like(mass_ref)
    for copy in copies:
        copy.wait()

    chip = me_ref[0]
    begins = []
    counts = []
    for p in range(plans):
        low = lists_ref[p, entries, chip] * 16 + lists_ref[p, entries, NC + chip]
        high = lists_ref[p, entries, chip + 1] * 16 + lists_ref[p, entries, NC + chip + 1]
        begins.append(low)
        counts.append(high - low)
    total = sum(counts)

    def task(k):
        k = jnp.minimum(k, total - 1)
        if plans == 1:
            late, at = 0, (k + begins[0]) * GROUP
        else:
            late = (k >= counts[0]).astype(jnp.int32)
            at = (k + begins[0] + late * (begins[1] - begins[0] - counts[0])) * GROUP
        at = jnp.maximum(at, 0)
        line, spot = lax.shift_right_logical(at, 7), at & 127
        words = [lists_ref[late, line, spot + g] for g in range(GROUP)]
        article = lax.shift_right_logical(words[0], 20) + late * articles
        rows = [(lax.shift_right_logical(w, bits) & 2047) + late * half for w in words]
        return article, [w & (2 * blocks - 1) for w in words], rows

    def block(c):
        spot = c & (blocks - 1)
        return jnp.where(c >= blocks, other_ref[spot], own_ref[spot])

    def some(step, carry):
        for u in range(UNROLL):
            article, picks, rows = task(step * UNROLL + u)
            chosen = jnp.concatenate([block(c) for c in picks], axis=0)
            sims = jnp.dot(chosen, turned_ref[article], preferred_element_type=jnp.float32)
            grown = jnp.exp2(sims * scale_ref[article][0:1])
            for g, row in enumerate(rows):
                mass_ref[pl.ds(row, 1), :] = jnp.sum(
                    grown[g * keys : (g + 1) * keys], axis=0, keepdims=True
                )
        return carry

    lax.fori_loop(0, (total + UNROLL - 1) // UNROLL, some, 0)

    per_home = articles // seqs
    lane = lax.broadcasted_iota(jnp.int32, (NC, 128), 1)
    for p in range(plans):
        sums = jnp.zeros((NC, 128), jnp.float32)
        for i in range(articles):
            logs = jnp.log2(mass_ref[p * half + i * NC : p * half + (i + 1) * NC, :])
            sums = jnp.where(lane == i, jnp.sum(logs, axis=1, keepdims=True), sums)
        out_refs[p][:, 0:NC] = (sums * (math.log(2) / SHARP)).T[0:articles]
    if not others:
        return

    spread_ref = out_refs[-1]
    spread_ref[...] = jnp.zeros_like(spread_ref)
    block_rows = spread_ref.shape[0] // (2 * chips * seqs)
    side, rest = chip & (wide - 1), chip >> (wide.bit_length() - 1)
    place = side * deep + jnp.where(side & 1 == 0, rest, deep - 1 - rest)
    spots = [0] + [x for d in range(1, chips // 2) for x in (-d, d)] + [chips // 2]
    for spot, ref in zip(spots, [*other_refs, out_refs[0]]):
        at = (place + spot + chips) & (chips - 1)
        side, rest = at >> (deep.bit_length() - 1), at & (deep - 1)
        home = jnp.where(side & 1 == 0, rest, deep - 1 - rest) * wide + side
        for k in range(seqs):
            peer = (2 * home + me_ref[1]) * seqs + k
            rows = pl.ds(pl.multiple_of(peer * block_rows, 8), per_home)
            spread_ref[rows, :] = ref[k * per_home : (k + 1) * per_home, :]


def score_chunks(me, pairs, far, others, own, other, tokens, wide, deep, seqs):
    chips = wide * deep
    plans = len(pairs)
    blocks, keys, width = own.shape
    articles = 2 * pairs[0][0].shape[0] // tokens
    shapes = [jax.ShapeDtypeStruct((articles, 128), jnp.float32)] * plans
    if others:
        rows = -(-(articles // seqs) // 8) * 8 * 2 * chips * seqs
        shapes.append(jax.ShapeDtypeStruct((rows, 128), jnp.float32))
    lines = -(-(plan_rows(chips, articles)[0] + 1) // 8) * 8
    work = plans * articles * 8
    smem, vmem = pl.BlockSpec(memory_space=pltpu.SMEM), pl.BlockSpec(memory_space=pltpu.VMEM)
    return pl.pallas_call(
        functools.partial(score_kernel, (plans, len(far), len(others), seqs, blocks, wide, deep)),
        out_shape=shapes,
        in_specs=[smem] + [vmem] * (2 * plans + len(far) + len(others) + 2),
        out_specs=[vmem] * len(shapes),
        scratch_shapes=[
            pltpu.VMEM((plans * articles, width, tokens), jnp.bfloat16),
            pltpu.VMEM((plans * articles, 8, tokens), jnp.float32),
            pltpu.VMEM((plans * (articles * NC + 8), tokens), jnp.float32),
            pltpu.VMEM((plans, lines, 128), jnp.int32),
            pltpu.SMEM((plans, lines, 128), jnp.int32),
            pltpu.SemaphoreType.DMA((plans,)),
        ],
        compiler_params=pltpu.CompilerParams(vmem_limit_bytes=32 * 1024 * 1024),
        cost_estimate=pl.CostEstimate(
            flops=int(SCOST * work * tokens * keys * width),
            bytes_accessed=4 * own.size,
            transcendentals=int(SCOST / 2 * work * tokens * keys),
        ),
        name="score_chunks",
    )(me, *[x for pair in pairs for x in pair], *far, *others, own, other)


def close_kernel(seqs, parts_ref, relevance_ref, probs_ref, score_ref):
    peers = parts_ref.shape[0]
    rows = relevance_ref.shape[0] // seqs
    for d in range(seqs):
        part = parts_ref[d]
        for j in range(d + seqs, peers, seqs):
            part = part + parts_ref[j]
        for i in range(rows):
            score_ref[i * seqs + d : i * seqs + d + 1, :] = part[i : i + 1]
    score = score_ref[:, 0:NC]
    relevance = score - jnp.mean(score, axis=-1, keepdims=True)
    weights = jnp.exp(TEMPER * relevance)
    relevance_ref[...] = relevance
    probs_ref[...] = weights / jnp.sum(weights, axis=-1, keepdims=True)


def close(parts, articles, seqs):
    vmem = pl.BlockSpec(memory_space=pltpu.VMEM)
    return pl.pallas_call(
        functools.partial(close_kernel, seqs),
        out_shape=[jax.ShapeDtypeStruct((articles, NC), jnp.float32)] * 2,
        in_specs=[vmem],
        out_specs=[vmem] * 2,
        scratch_shapes=[pltpu.VMEM((articles, 128), jnp.float32)],
        name="close",
    )(parts)


def per_device(wide, deep, queries, cand_owner, cand_local, companies):
    articles = queries.shape[0]
    seqs, arts = lax.axis_size("seq"), lax.axis_size("art")
    art, seq = lax.axis_index("art"), lax.axis_index("seq")
    chips = wide * deep
    half = chips // 2
    per_home = articles // seqs
    blocks = companies.shape[0]
    tokens = queries.shape[2]
    mine = queries.reshape(articles * tokens, queries.shape[3])
    ring = []
    for y in range(wide):
        for z in range(deep) if y % 2 == 0 else reversed(range(deep)):
            ring.append(z * wide + y)

    def turn(step, across=0):
        return [
            (
                (2 * ring[i] + c) * seqs + s,
                (2 * ring[(i + step) % chips] + c) * seqs + (s + across) % seqs,
            )
            for i in range(chips)
            for c in range(2)
            for s in range(seqs)
        ]

    def send(array, step, across=0):
        return lax.ppermute(array, ("art", "seq"), turn(step, across))

    cut = articles // 2 * tokens
    one, rest = mine[:cut], mine[cut:]
    ahead, behind = [None], [None]
    first = [send(one, 1), send(rest, -1)]

    ids = (cand_owner * blocks + cand_local).reshape(per_home, seqs * NC)
    ids = [ids] + [send(ids, 0, d) for d in range(1, seqs)]
    me = jnp.stack([art // 2, art % 2, seq]).astype(jnp.int32)
    two, back, lists = pack_streams(me, ids, one, rest, chips, blocks)
    second = [send(two, 1), send(back, -1)]
    ahead.append([first[0], second[0]])
    behind.append([first[1], second[1]])
    own = unit_blocks(lax.optimization_barrier((companies, *first))[0])
    other = lax.ppermute(companies, "art", [(i, i ^ 1) for i in range(arts)])
    other = unit_blocks(lax.optimization_barrier((other, *first))[0])

    def score(*pairs, far=(), others=()):
        return score_chunks(me, pairs, far, others, own, other, tokens, wide, deep, seqs)

    def after(array, *things):
        return lax.optimization_barrier((array, *things))[0]

    early = list(score((after(one, *second), two)))
    done = early[0]
    far = send(after(lists, done), half)
    for d in range(1, half):
        a, b = [ahead[d][0], behind[d][0]], [ahead[d][1], behind[d][1]]
        if d == 1:
            b = [after(x, own) for x in b]
        else:
            fresh = after(ahead[d - 1][0], done, *a, *([far] if d == 3 else []))
            more = score((fresh, ahead[d - 1][1]), behind[d - 1])
            early += more
            a = [after(x, done if d + 1 < half else more[0]) for x in a]
            b = [after(x, more[0]) for x in b]
            done = more[0]
        a, b = lax.optimization_barrier(a), lax.optimization_barrier(b)
        if d + 1 < half:
            ahead.append([send(a[0], 1), send(b[0], 1)])
            behind.append([send(a[1], -1), send(b[1], -1)])
        else:
            ahead[d][0] = a[0]
            last = (send(a[0], 1), send(a[1], -1))
    early += score(ahead[half - 1], behind[half - 1])
    spread = score(last, far=(far,), others=early)[1]
    parts = lax.all_to_all(spread, ("art", "seq"), split_axis=0, concat_axis=0, tiled=True)
    return tuple(close(parts.reshape(arts * seqs, -1, 128), articles, seqs))


def solution(mesh):
    chips = mesh.shape["art"] // 2
    wide = math.gcd(mesh.shape["seq"], chips)
    placed = (
        P("art", "seq", None, None),
        P(("art", "seq"), None, None),
        P(("art", "seq"), None, None),
        P("art", None, None),
    )
    return jax.shard_map(
        functools.partial(per_device, wide, chips // wide),
        mesh=mesh,
        in_specs=placed,
        out_specs=(P(("art", "seq"), None), P(("art", "seq"), None)),
        check_vma=False,
    )
```

```python
import functools
import math

import jax
import jax.numpy as jnp
from jax import lax
from jax.experimental import pallas as pl
from jax.experimental.pallas import tpu as pltpu
from jax.sharding import PartitionSpec as P

NC = 64
EPS = 1e-06
SHARP = 16.0
TEMPER = 4.0
GROUP = 4
UCOST = 4000000000
SCOST = 2.0
UNROLL = 20
PREP = 3
LAST = (((1,), (1,)), ((), ()))


def unit_kernel(parts, blocks_ref, out_ref, held_ref, sems):
    part = blocks_ref.shape[0] // parts
    copies = []
    for p in range(parts):
        rows = pl.ds(p * part, part)
        copies.append(pltpu.make_async_copy(blocks_ref.at[rows], held_ref.at[rows], sems.at[p]))
        copies[-1].start()
    for p in range(parts):
        copies[p].wait()

        def some(i, carry, p=p):
            rows = pl.ds(p * part + 2 * i, 2)
            wide = held_ref[rows].astype(jnp.float32)
            norm = jnp.sum(wide * wide, axis=-1, keepdims=True)
            out_ref[rows] = (wide * lax.rsqrt(norm + EPS)).astype(jnp.bfloat16)
            return carry

        lax.fori_loop(0, part // 2, some, 0, unroll=16)


def unit_blocks(blocks):
    parts = 4
    return pl.pallas_call(
        functools.partial(unit_kernel, parts),
        out_shape=jax.ShapeDtypeStruct(blocks.shape, jnp.bfloat16),
        in_specs=[pl.BlockSpec(memory_space=pltpu.HBM)],
        out_specs=pl.BlockSpec(memory_space=pltpu.VMEM),
        scratch_shapes=[
            pltpu.VMEM(blocks.shape, jnp.bfloat16),
            pltpu.SemaphoreType.DMA((parts,)),
        ],
        compiler_params=pltpu.CompilerParams(vmem_limit_bytes=32 * 1024 * 1024),
        cost_estimate=pl.CostEstimate(flops=UCOST, bytes_accessed=1, transcendentals=0),
        name="unit_blocks",
    )(pltpu.with_memory_space_constraint(blocks, pltpu.HBM))


def mask(m):
    return m.astype(jnp.float32).astype(jnp.bfloat16)


def plan_rows(chips, articles):
    entries = -(-(articles * NC + chips * articles * (GROUP - 1)) // 128)
    return entries, -(-(3 * entries + 1) // 16) * 16


def pack_kernel(chips, blocks, me_ref, *refs):
    id_refs, (first_ref, second_ref, ahead_ref, behind_ref, lists_ref) = refs[:-5], refs[-5:]
    seqs = len(id_refs)
    core, seq = me_ref[1], me_ref[2]
    per_home, width = id_refs[0].shape
    rows = first_ref.shape[0]
    ahead_ref[0:rows, :] = second_ref[...]
    behind_ref[0:rows, :] = first_ref[...]

    lane = lax.broadcasted_iota(jnp.int32, (per_home, width), 1)
    ids = jnp.zeros((per_home, width), jnp.int32)
    for d in range(seqs):
        table = id_refs[d][...]
        for p in range(seqs):
            k = (p + seqs - d) % seqs
            turned = table if k == p else pltpu.roll(table, (k - p) % seqs * NC, 1)
            ids = jnp.where((seq == p) & (lane // NC == k), turned, ids)
    ids = jnp.concatenate([ids[i : i + 1] for i in range(per_home)], axis=1)
    lanes = per_home * width
    articles = lanes // NC
    owner, local = ids // blocks, ids % blocks
    other = jnp.where(owner % 2 != core, 1, 0)
    here = owner // 2 == lax.broadcasted_iota(jnp.int32, (chips, lanes), 0)
    hot = mask(here)
    a = lax.broadcasted_iota(jnp.int32, (lanes, lanes), 0)
    b = lax.broadcasted_iota(jnp.int32, (lanes, lanes), 1)
    same = a // NC == b // NC
    rank = jnp.dot(hot, mask(same & (a <= b)), preferred_element_type=jnp.float32)
    amount = jnp.dot(hot, mask(same), preferred_element_type=jnp.float32).astype(jnp.int32)
    groups = (amount + (GROUP - 1)) // GROUP
    lead = lax.broadcasted_iota(jnp.int32, (chips, lanes), 1) % NC == 0
    tops = jnp.where(lead, groups, 0).astype(jnp.float32)
    ahead = jnp.dot(
        tops.astype(jnp.bfloat16), mask(a // NC < b // NC), preferred_element_type=jnp.float32
    )
    totals = jnp.sum(tops, axis=1, keepdims=True)
    lane = lax.broadcasted_iota(jnp.int32, (chips, 128), 1)
    before = lax.broadcasted_iota(jnp.int32, (chips, 128), 0) < lane % NC
    starts = jnp.sum(jnp.where(before, totals, 0.0), axis=0, keepdims=True).astype(jnp.int32)
    starts = jnp.where(lane[0:1] < NC, starts // 16, starts % 16).astype(jnp.float32)
    fence = mask(
        lax.broadcasted_iota(jnp.int32, (chips, chips), 1)
        < lax.broadcasted_iota(jnp.int32, (chips, chips), 0)
    )
    base = jnp.dot(fence, tops.astype(jnp.bfloat16), preferred_element_type=jnp.float32)
    base = jnp.sum(base, axis=1, keepdims=True)
    spot = jnp.where(here, GROUP * (base + ahead) + rank - 1.0, 0.0)
    spot = jnp.sum(spot, axis=0, keepdims=True).astype(jnp.int32)
    lane = lax.broadcasted_iota(jnp.int32, (1, lanes), 1)
    article = lane // NC % seqs * per_home + lane // width
    kinds = lax.broadcasted_iota(jnp.int32, (8, lanes), 0)
    fields = jnp.ones((8, lanes), jnp.int32)
    for k, row in enumerate((local, other * 128 + lane % NC, article)):
        fields = jnp.where(kinds == k, row, fields)
    entries, extra = plan_rows(chips, articles)
    slots = lax.broadcasted_iota(jnp.int32, (entries * 128, lanes), 0)
    got = lax.dot_general(
        fields.astype(jnp.float32).astype(jnp.bfloat16),
        mask(slots == spot),
        LAST,
        preferred_element_type=jnp.float32,
    )
    code = jnp.where(got[3:4] > 0.5, got[1:2], float(NC))
    lists = jnp.concatenate([got[0:1], code, got[2:3]], axis=1)
    lists = [lists[:, i * 128 : (i + 1) * 128] for i in range(3 * entries)]
    lists += [starts, jnp.zeros((extra - 3 * entries - 1, 128), jnp.float32)]
    lists = jnp.concatenate(lists, axis=0).astype(jnp.bfloat16)
    ahead_ref[rows : rows + extra, :] = lists
    behind_ref[rows : rows + extra, :] = lists
    lists_ref[...] = lists


def pack_streams(me, ids, first, second, chips, blocks):
    vmem = pl.BlockSpec(memory_space=pltpu.VMEM)
    articles = len(ids) * ids[0].shape[0]
    extra = plan_rows(chips, articles)[1]
    shapes = [(first.shape[0] + extra, first.shape[1])] * 2 + [(extra, first.shape[1])]
    return pl.pallas_call(
        functools.partial(pack_kernel, chips, blocks),
        out_shape=[jax.ShapeDtypeStruct(shape, jnp.bfloat16) for shape in shapes],
        in_specs=[pl.BlockSpec(memory_space=pltpu.SMEM)] + [vmem] * (len(ids) + 2),
        out_specs=[vmem] * 3,
        compiler_params=pltpu.CompilerParams(vmem_limit_bytes=32 * 1024 * 1024),
        cost_estimate=pl.CostEstimate(flops=1, bytes_accessed=1, transcendentals=0),
        name="pack_streams",
    )(me, *ids, first, second)


def score_kernel(dims, me_ref, *refs):
    plans, apart, others, seqs, blocks, wide, deep = dims
    chips = wide * deep
    pair_refs, refs = refs[: 2 * plans], refs[2 * plans :]
    far_refs, refs = refs[:apart], refs[apart:]
    other_refs, refs = refs[:others], refs[others:]
    own_ref, other_ref, *refs = refs
    out_refs = refs[:-6]
    turned_ref, scale_ref, mass_ref, words_ref, lists_ref, sems = refs[-6:]
    articles = turned_ref.shape[0] // plans
    tokens = mass_ref.shape[1]
    keys = own_ref.shape[1]
    half = mass_ref.shape[0] // plans
    entries, extra = plan_rows(chips, articles)
    bits = (2 * blocks - 1).bit_length()
    begin = articles // 2 * tokens

    copies = []
    for p in range(plans):
        rows = far_refs[0][...] if apart else pair_refs[2 * p + 1][begin : begin + extra, :]
        rows = rows.astype(jnp.float32).astype(jnp.int32)
        local, code, article, starts = (rows[k * entries : (k + 1) * entries] for k in range(4))
        place = code % 128
        row = jnp.where(place < NC, article * NC + place, articles * NC)
        word = local + blocks * (code // 128) + 2 * blocks * row + (1 << 20) * article
        words_ref[p, 0:entries, :] = word
        words_ref[p, entries : entries + 1, :] = starts[0:1]
        copy = pltpu.make_async_copy(words_ref.at[p], lists_ref.at[p], sems.at[p])
        copy.start()
        copies.append(copy)

    def prepare(i, carry):
        for p, ref in enumerate(pair_refs):
            query = ref[pl.ds(pl.multiple_of(i * tokens, tokens), tokens), :]
            wide = query.astype(jnp.float32)
            norm = lax.dot_general(
                jnp.ones((8, query.shape[1]), jnp.bfloat16),
                (wide * wide).astype(jnp.bfloat16),
                LAST,
                preferred_element_type=jnp.float32,
            )
            late = p % 2 if p < 2 else 1 - p % 2
            at = p // 2 * articles + late * (articles // 2) + i
            scale_ref[at] = lax.rsqrt(norm + EPS) * (SHARP * math.log2(math.e))
            turned_ref[at] = query.T
        return carry

    lax.fori_loop(0, articles // 2, prepare, 0, unroll=PREP)
    mass_ref[...] = jnp.ones_like(mass_ref)
    for copy in copies:
        copy.wait()

    chip = me_ref[0]
    begins = []
    counts = []
    for p in range(plans):
        low = lists_ref[p, entries, chip] * 16 + lists_ref[p, entries, NC + chip]
        high = lists_ref[p, entries, chip + 1] * 16 + lists_ref[p, entries, NC + chip + 1]
        begins.append(low)
        counts.append(high - low)
    total = sum(counts)

    def task(k):
        k = jnp.minimum(k, total - 1)
        if plans == 1:
            late, at = 0, (k + begins[0]) * GROUP
        else:
            late = (k >= counts[0]).astype(jnp.int32)
            at = (k + begins[0] + late * (begins[1] - begins[0] - counts[0])) * GROUP
        at = jnp.maximum(at, 0)
        line, spot = lax.shift_right_logical(at, 7), at & 127
        words = [lists_ref[late, line, spot + g] for g in range(GROUP)]
        article = lax.shift_right_logical(words[0], 20) + late * articles
        rows = [(lax.shift_right_logical(w, bits) & 2047) + late * half for w in words]
        return article, [w & (2 * blocks - 1) for w in words], rows

    def block(c):
        spot = c & (blocks - 1)
        return jnp.where(c >= blocks, other_ref[spot], own_ref[spot])

    def some(step, carry):
        for u in range(UNROLL):
            article, picks, rows = task(step * UNROLL + u)
            chosen = jnp.concatenate([block(c) for c in picks], axis=0)
            sims = jnp.dot(chosen, turned_ref[article], preferred_element_type=jnp.float32)
            grown = jnp.exp2(sims * scale_ref[article][0:1])
            for g, row in enumerate(rows):
                mass_ref[pl.ds(row, 1), :] = jnp.sum(
                    grown[g * keys : (g + 1) * keys], axis=0, keepdims=True
                )
        return carry

    lax.fori_loop(0, (total + UNROLL - 1) // UNROLL, some, 0)

    per_home = articles // seqs
    lane = lax.broadcasted_iota(jnp.int32, (NC, 128), 1)
    for p in range(plans):
        sums = jnp.zeros((NC, 128), jnp.float32)
        for i in range(articles):
            logs = jnp.log2(mass_ref[p * half + i * NC : p * half + (i + 1) * NC, :])
            sums = jnp.where(lane == i, jnp.sum(logs, axis=1, keepdims=True), sums)
        out_refs[p][:, 0:NC] = (sums * (math.log(2) / SHARP)).T[0:articles]
    if not others:
        return

    spread_ref = out_refs[-1]
    spread_ref[...] = jnp.zeros_like(spread_ref)
    block_rows = spread_ref.shape[0] // (2 * chips * seqs)
    side, rest = chip & (wide - 1), chip >> (wide.bit_length() - 1)
    place = side * deep + jnp.where(side & 1 == 0, rest, deep - 1 - rest)
    spots = [0] + [x for d in range(1, chips // 2) for x in (-d, d)] + [chips // 2]
    for spot, ref in zip(spots, [*other_refs, out_refs[0]]):
        at = (place + spot + chips) & (chips - 1)
        side, rest = at >> (deep.bit_length() - 1), at & (deep - 1)
        home = jnp.where(side & 1 == 0, rest, deep - 1 - rest) * wide + side
        for k in range(seqs):
            peer = (2 * home + me_ref[1]) * seqs + k
            rows = pl.ds(pl.multiple_of(peer * block_rows, 8), per_home)
            spread_ref[rows, :] = ref[k * per_home : (k + 1) * per_home, :]


def score_chunks(me, pairs, far, others, own, other, tokens, wide, deep, seqs):
    chips = wide * deep
    plans = len(pairs)
    blocks, keys, width = own.shape
    articles = 2 * pairs[0][0].shape[0] // tokens
    shapes = [jax.ShapeDtypeStruct((articles, 128), jnp.float32)] * plans
    if others:
        rows = -(-(articles // seqs) // 8) * 8 * 2 * chips * seqs
        shapes.append(jax.ShapeDtypeStruct((rows, 128), jnp.float32))
    lines = -(-(plan_rows(chips, articles)[0] + 1) // 8) * 8
    work = plans * articles * 8
    smem, vmem = pl.BlockSpec(memory_space=pltpu.SMEM), pl.BlockSpec(memory_space=pltpu.VMEM)
    return pl.pallas_call(
        functools.partial(score_kernel, (plans, len(far), len(others), seqs, blocks, wide, deep)),
        out_shape=shapes,
        in_specs=[smem] + [vmem] * (2 * plans + len(far) + len(others) + 2),
        out_specs=[vmem] * len(shapes),
        scratch_shapes=[
            pltpu.VMEM((plans * articles, width, tokens), jnp.bfloat16),
            pltpu.VMEM((plans * articles, 8, tokens), jnp.float32),
            pltpu.VMEM((plans * (articles * NC + 8), tokens), jnp.float32),
            pltpu.VMEM((plans, lines, 128), jnp.int32),
            pltpu.SMEM((plans, lines, 128), jnp.int32),
            pltpu.SemaphoreType.DMA((plans,)),
        ],
        compiler_params=pltpu.CompilerParams(vmem_limit_bytes=32 * 1024 * 1024),
        cost_estimate=pl.CostEstimate(
            flops=int(SCOST * work * tokens * keys * width),
            bytes_accessed=4 * own.size,
            transcendentals=int(SCOST / 2 * work * tokens * keys),
        ),
        name="score_chunks",
    )(me, *[x for pair in pairs for x in pair], *far, *others, own, other)


def close_kernel(seqs, parts_ref, relevance_ref, probs_ref, score_ref):
    peers = parts_ref.shape[0]
    rows = relevance_ref.shape[0] // seqs
    for d in range(seqs):
        part = parts_ref[d]
        for j in range(d + seqs, peers, seqs):
            part = part + parts_ref[j]
        for i in range(rows):
            score_ref[i * seqs + d : i * seqs + d + 1, :] = part[i : i + 1]
    score = score_ref[:, 0:NC]
    relevance = score - jnp.mean(score, axis=-1, keepdims=True)
    weights = jnp.exp(TEMPER * relevance)
    relevance_ref[...] = relevance
    probs_ref[...] = weights / jnp.sum(weights, axis=-1, keepdims=True)


def close(parts, articles, seqs):
    vmem = pl.BlockSpec(memory_space=pltpu.VMEM)
    return pl.pallas_call(
        functools.partial(close_kernel, seqs),
        out_shape=[jax.ShapeDtypeStruct((articles, NC), jnp.float32)] * 2,
        in_specs=[vmem],
        out_specs=[vmem] * 2,
        scratch_shapes=[pltpu.VMEM((articles, 128), jnp.float32)],
        name="close",
    )(parts)


def per_device(wide, deep, queries, cand_owner, cand_local, companies):
    articles = queries.shape[0]
    seqs, arts = lax.axis_size("seq"), lax.axis_size("art")
    art, seq = lax.axis_index("art"), lax.axis_index("seq")
    chips = wide * deep
    half = chips // 2
    per_home = articles // seqs
    blocks = companies.shape[0]
    tokens = queries.shape[2]
    mine = queries.reshape(articles * tokens, queries.shape[3])
    ring = []
    for y in range(wide):
        for z in range(deep) if y % 2 == 0 else reversed(range(deep)):
            ring.append(z * wide + y)

    def turn(step, across=0):
        return [
            (
                (2 * ring[i] + c) * seqs + s,
                (2 * ring[(i + step) % chips] + c) * seqs + (s + across) % seqs,
            )
            for i in range(chips)
            for c in range(2)
            for s in range(seqs)
        ]

    def send(array, step, across=0):
        return lax.ppermute(array, ("art", "seq"), turn(step, across))

    cut = articles // 2 * tokens
    one, rest = mine[:cut], mine[cut:]
    ahead, behind = [None], [None]
    first = [send(one, 1), send(rest, -1)]

    ids = (cand_owner * blocks + cand_local).reshape(per_home, seqs * NC)
    ids = [ids] + [send(ids, 0, d) for d in range(1, seqs)]
    me = jnp.stack([art // 2, art % 2, seq]).astype(jnp.int32)
    two, back, lists = pack_streams(me, ids, one, rest, chips, blocks)
    second = [send(two, 1), send(back, -1)]
    ahead.append([first[0], second[0]])
    behind.append([first[1], second[1]])
    own = unit_blocks(lax.optimization_barrier((companies, *first))[0])
    other = lax.ppermute(companies, "art", [(i, i ^ 1) for i in range(arts)])
    other = unit_blocks(lax.optimization_barrier((other, *first))[0])

    def score(*pairs, far=(), others=()):
        return score_chunks(me, pairs, far, others, own, other, tokens, wide, deep, seqs)

    def after(array, *things):
        return lax.optimization_barrier((array, *things))[0]

    early = list(score((after(one, *second), two)))
    done = early[0]
    far = send(after(lists, done), half)
    for d in range(1, half):
        a, b = [ahead[d][0], behind[d][0]], [ahead[d][1], behind[d][1]]
        if d == 1:
            b = [after(x, own) for x in b]
        else:
            fresh = after(ahead[d - 1][0], done, *a, *([far] if d == 3 else []))
            more = score((fresh, ahead[d - 1][1]), behind[d - 1])
            early += more
            a = [after(x, done if d + 1 < half else more[0]) for x in a]
            b = [after(x, more[0]) for x in b]
            done = more[0]
        a, b = lax.optimization_barrier(a), lax.optimization_barrier(b)
        if d + 1 < half:
            ahead.append([send(a[0], 1), send(b[0], 1)])
            behind.append([send(a[1], -1), send(b[1], -1)])
        else:
            ahead[d][0] = a[0]
            last = (send(a[0], 1), send(a[1], -1))
    early += score(ahead[half - 1], behind[half - 1])
    spread = score(last, far=(far,), others=early)[1]
    parts = lax.all_to_all(spread, ("art", "seq"), split_axis=0, concat_axis=0, tiled=True)
    return tuple(close(parts.reshape(arts * seqs, -1, 128), articles, seqs))


def solution(mesh):
    chips = mesh.shape["art"] // 2
    wide = math.gcd(mesh.shape["seq"], chips)
    placed = (
        P("art", "seq", None, None),
        P(("art", "seq"), None, None),
        P(("art", "seq"), None, None),
        P("art", None, None),
    )
    return jax.shard_map(
        functools.partial(per_device, wide, chips // wide),
        mesh=mesh,
        in_specs=placed,
        out_specs=(P(("art", "seq"), None), P(("art", "seq"), None)),
        check_vma=False,
    )
```

```python
import functools
import math

import jax
import jax.numpy as jnp
from jax import lax
from jax.experimental import pallas as pl
from jax.experimental.pallas import tpu as pltpu
from jax.sharding import PartitionSpec as P

NC = 64
EPS = 1e-06
SHARP = 16.0
TEMPER = 4.0
GROUP = 4
UCOST = 4000000000
SCOST = 2.0
UNROLL = 24
PREP = 3
LAST = (((1,), (1,)), ((), ()))


def unit_kernel(parts, blocks_ref, out_ref, held_ref, sems):
    part = blocks_ref.shape[0] // parts
    copies = []
    for p in range(parts):
        rows = pl.ds(p * part, part)
        copies.append(pltpu.make_async_copy(blocks_ref.at[rows], held_ref.at[rows], sems.at[p]))
        copies[-1].start()
    for p in range(parts):
        copies[p].wait()

        def some(i, carry, p=p):
            rows = pl.ds(p * part + 2 * i, 2)
            wide = held_ref[rows].astype(jnp.float32)
            norm = jnp.sum(wide * wide, axis=-1, keepdims=True)
            out_ref[rows] = (wide * lax.rsqrt(norm + EPS)).astype(jnp.bfloat16)
            return carry

        lax.fori_loop(0, part // 2, some, 0, unroll=16)


def unit_blocks(blocks):
    parts = 4
    return pl.pallas_call(
        functools.partial(unit_kernel, parts),
        out_shape=jax.ShapeDtypeStruct(blocks.shape, jnp.bfloat16),
        in_specs=[pl.BlockSpec(memory_space=pltpu.HBM)],
        out_specs=pl.BlockSpec(memory_space=pltpu.VMEM),
        scratch_shapes=[
            pltpu.VMEM(blocks.shape, jnp.bfloat16),
            pltpu.SemaphoreType.DMA((parts,)),
        ],
        compiler_params=pltpu.CompilerParams(vmem_limit_bytes=32 * 1024 * 1024),
        cost_estimate=pl.CostEstimate(flops=UCOST, bytes_accessed=1, transcendentals=0),
        name="unit_blocks",
    )(pltpu.with_memory_space_constraint(blocks, pltpu.HBM))


def mask(m):
    return m.astype(jnp.float32).astype(jnp.bfloat16)


def plan_rows(chips, articles):
    entries = -(-(articles * NC + chips * articles * (GROUP - 1)) // 128)
    return entries, -(-(3 * entries + 1) // 16) * 16


def pack_kernel(chips, blocks, me_ref, *refs):
    id_refs, (first_ref, second_ref, ahead_ref, behind_ref, lists_ref) = refs[:-5], refs[-5:]
    seqs = len(id_refs)
    core, seq = me_ref[1], me_ref[2]
    per_home, width = id_refs[0].shape
    rows = first_ref.shape[0]
    ahead_ref[0:rows, :] = second_ref[...]
    behind_ref[0:rows, :] = first_ref[...]

    lane = lax.broadcasted_iota(jnp.int32, (per_home, width), 1)
    ids = jnp.zeros((per_home, width), jnp.int32)
    for d in range(seqs):
        table = id_refs[d][...]
        for p in range(seqs):
            k = (p + seqs - d) % seqs
            turned = table if k == p else pltpu.roll(table, (k - p) % seqs * NC, 1)
            ids = jnp.where((seq == p) & (lane // NC == k), turned, ids)
    ids = jnp.concatenate([ids[i : i + 1] for i in range(per_home)], axis=1)
    lanes = per_home * width
    articles = lanes // NC
    owner, local = ids // blocks, ids % blocks
    other = jnp.where(owner % 2 != core, 1, 0)
    here = owner // 2 == lax.broadcasted_iota(jnp.int32, (chips, lanes), 0)
    hot = mask(here)
    a = lax.broadcasted_iota(jnp.int32, (lanes, lanes), 0)
    b = lax.broadcasted_iota(jnp.int32, (lanes, lanes), 1)
    same = a // NC == b // NC
    rank = jnp.dot(hot, mask(same & (a <= b)), preferred_element_type=jnp.float32)
    amount = jnp.dot(hot, mask(same), preferred_element_type=jnp.float32).astype(jnp.int32)
    groups = (amount + (GROUP - 1)) // GROUP
    lead = lax.broadcasted_iota(jnp.int32, (chips, lanes), 1) % NC == 0
    tops = jnp.where(lead, groups, 0).astype(jnp.float32)
    ahead = jnp.dot(
        tops.astype(jnp.bfloat16), mask(a // NC < b // NC), preferred_element_type=jnp.float32
    )
    totals = jnp.sum(tops, axis=1, keepdims=True)
    lane = lax.broadcasted_iota(jnp.int32, (chips, 128), 1)
    before = lax.broadcasted_iota(jnp.int32, (chips, 128), 0) < lane % NC
    starts = jnp.sum(jnp.where(before, totals, 0.0), axis=0, keepdims=True).astype(jnp.int32)
    starts = jnp.where(lane[0:1] < NC, starts // 16, starts % 16).astype(jnp.float32)
    fence = mask(
        lax.broadcasted_iota(jnp.int32, (chips, chips), 1)
        < lax.broadcasted_iota(jnp.int32, (chips, chips), 0)
    )
    base = jnp.dot(fence, tops.astype(jnp.bfloat16), preferred_element_type=jnp.float32)
    base = jnp.sum(base, axis=1, keepdims=True)
    spot = jnp.where(here, GROUP * (base + ahead) + rank - 1.0, 0.0)
    spot = jnp.sum(spot, axis=0, keepdims=True).astype(jnp.int32)
    lane = lax.broadcasted_iota(jnp.int32, (1, lanes), 1)
    article = lane // NC % seqs * per_home + lane // width
    kinds = lax.broadcasted_iota(jnp.int32, (8, lanes), 0)
    fields = jnp.ones((8, lanes), jnp.int32)
    for k, row in enumerate((local, other * 128 + lane % NC, article)):
        fields = jnp.where(kinds == k, row, fields)
    entries, extra = plan_rows(chips, articles)
    slots = lax.broadcasted_iota(jnp.int32, (entries * 128, lanes), 0)
    got = lax.dot_general(
        fields.astype(jnp.float32).astype(jnp.bfloat16),
        mask(slots == spot),
        LAST,
        preferred_element_type=jnp.float32,
    )
    code = jnp.where(got[3:4] > 0.5, got[1:2], float(NC))
    lists = jnp.concatenate([got[0:1], code, got[2:3]], axis=1)
    lists = [lists[:, i * 128 : (i + 1) * 128] for i in range(3 * entries)]
    lists += [starts, jnp.zeros((extra - 3 * entries - 1, 128), jnp.float32)]
    lists = jnp.concatenate(lists, axis=0).astype(jnp.bfloat16)
    ahead_ref[rows : rows + extra, :] = lists
    behind_ref[rows : rows + extra, :] = lists
    lists_ref[...] = lists


def pack_streams(me, ids, first, second, chips, blocks):
    vmem = pl.BlockSpec(memory_space=pltpu.VMEM)
    articles = len(ids) * ids[0].shape[0]
    extra = plan_rows(chips, articles)[1]
    shapes = [(first.shape[0] + extra, first.shape[1])] * 2 + [(extra, first.shape[1])]
    return pl.pallas_call(
        functools.partial(pack_kernel, chips, blocks),
        out_shape=[jax.ShapeDtypeStruct(shape, jnp.bfloat16) for shape in shapes],
        in_specs=[pl.BlockSpec(memory_space=pltpu.SMEM)] + [vmem] * (len(ids) + 2),
        out_specs=[vmem] * 3,
        compiler_params=pltpu.CompilerParams(vmem_limit_bytes=32 * 1024 * 1024),
        cost_estimate=pl.CostEstimate(flops=1, bytes_accessed=1, transcendentals=0),
        name="pack_streams",
    )(me, *ids, first, second)


def score_kernel(dims, me_ref, *refs):
    plans, apart, others, seqs, blocks, wide, deep = dims
    chips = wide * deep
    pair_refs, refs = refs[: 2 * plans], refs[2 * plans :]
    far_refs, refs = refs[:apart], refs[apart:]
    other_refs, refs = refs[:others], refs[others:]
    own_ref, other_ref, *refs = refs
    out_refs = refs[:-6]
    turned_ref, scale_ref, mass_ref, words_ref, lists_ref, sems = refs[-6:]
    articles = turned_ref.shape[0] // plans
    tokens = mass_ref.shape[1]
    keys = own_ref.shape[1]
    half = mass_ref.shape[0] // plans
    entries, extra = plan_rows(chips, articles)
    bits = (2 * blocks - 1).bit_length()
    begin = articles // 2 * tokens

    copies = []
    for p in range(plans):
        rows = far_refs[0][...] if apart else pair_refs[2 * p + 1][begin : begin + extra, :]
        rows = rows.astype(jnp.float32).astype(jnp.int32)
        local, code, article, starts = (rows[k * entries : (k + 1) * entries] for k in range(4))
        place = code % 128
        row = jnp.where(place < NC, article * NC + place, articles * NC)
        word = local + blocks * (code // 128) + 2 * blocks * row + (1 << 20) * article
        words_ref[p, 0:entries, :] = word
        words_ref[p, entries : entries + 1, :] = starts[0:1]
        copy = pltpu.make_async_copy(words_ref.at[p], lists_ref.at[p], sems.at[p])
        copy.start()
        copies.append(copy)

    def prepare(i, carry):
        for p, ref in enumerate(pair_refs):
            query = ref[pl.ds(pl.multiple_of(i * tokens, tokens), tokens), :]
            wide = query.astype(jnp.float32)
            norm = lax.dot_general(
                jnp.ones((8, query.shape[1]), jnp.bfloat16),
                (wide * wide).astype(jnp.bfloat16),
                LAST,
                preferred_element_type=jnp.float32,
            )
            late = p % 2 if p < 2 else 1 - p % 2
            at = p // 2 * articles + late * (articles // 2) + i
            scale_ref[at] = lax.rsqrt(norm + EPS) * (SHARP * math.log2(math.e))
            turned_ref[at] = query.T
        return carry

    lax.fori_loop(0, articles // 2, prepare, 0, unroll=PREP)
    mass_ref[...] = jnp.ones_like(mass_ref)
    for copy in copies:
        copy.wait()

    chip = me_ref[0]
    begins = []
    counts = []
    for p in range(plans):
        low = lists_ref[p, entries, chip] * 16 + lists_ref[p, entries, NC + chip]
        high = lists_ref[p, entries, chip + 1] * 16 + lists_ref[p, entries, NC + chip + 1]
        begins.append(low)
        counts.append(high - low)
    total = sum(counts)

    def task(k):
        k = jnp.minimum(k, total - 1)
        if plans == 1:
            late, at = 0, (k + begins[0]) * GROUP
        else:
            late = (k >= counts[0]).astype(jnp.int32)
            at = (k + begins[0] + late * (begins[1] - begins[0] - counts[0])) * GROUP
        at = jnp.maximum(at, 0)
        line, spot = lax.shift_right_logical(at, 7), at & 127
        words = [lists_ref[late, line, spot + g] for g in range(GROUP)]
        article = lax.shift_right_logical(words[0], 20) + late * articles
        rows = [(lax.shift_right_logical(w, bits) & 2047) + late * half for w in words]
        return article, [w & (2 * blocks - 1) for w in words], rows

    def block(c):
        spot = c & (blocks - 1)
        return jnp.where(c >= blocks, other_ref[spot], own_ref[spot])

    def some(step, carry):
        for u in range(UNROLL):
            article, picks, rows = task(step * UNROLL + u)
            chosen = jnp.concatenate([block(c) for c in picks], axis=0)
            sims = jnp.dot(chosen, turned_ref[article], preferred_element_type=jnp.float32)
            grown = jnp.exp2(sims * scale_ref[article][0:1])
            for g, row in enumerate(rows):
                mass_ref[pl.ds(row, 1), :] = jnp.sum(
                    grown[g * keys : (g + 1) * keys], axis=0, keepdims=True
                )
        return carry

    lax.fori_loop(0, (total + UNROLL - 1) // UNROLL, some, 0)

    per_home = articles // seqs
    lane = lax.broadcasted_iota(jnp.int32, (NC, 128), 1)
    for p in range(plans):
        sums = jnp.zeros((NC, 128), jnp.float32)
        for i in range(articles):
            logs = jnp.log2(mass_ref[p * half + i * NC : p * half + (i + 1) * NC, :])
            sums = jnp.where(lane == i, jnp.sum(logs, axis=1, keepdims=True), sums)
        out_refs[p][:, 0:NC] = (sums * (math.log(2) / SHARP)).T[0:articles]
    if not others:
        return

    spread_ref = out_refs[-1]
    spread_ref[...] = jnp.zeros_like(spread_ref)
    block_rows = spread_ref.shape[0] // (2 * chips * seqs)
    side, rest = chip & (wide - 1), chip >> (wide.bit_length() - 1)
    place = side * deep + jnp.where(side & 1 == 0, rest, deep - 1 - rest)
    spots = [0] + [x for d in range(1, chips // 2) for x in (-d, d)] + [chips // 2]
    for spot, ref in zip(spots, [*other_refs, out_refs[0]]):
        at = (place + spot + chips) & (chips - 1)
        side, rest = at >> (deep.bit_length() - 1), at & (deep - 1)
        home = jnp.where(side & 1 == 0, rest, deep - 1 - rest) * wide + side
        for k in range(seqs):
            peer = (2 * home + me_ref[1]) * seqs + k
            rows = pl.ds(pl.multiple_of(peer * block_rows, 8), per_home)
            spread_ref[rows, :] = ref[k * per_home : (k + 1) * per_home, :]


def score_chunks(me, pairs, far, others, own, other, tokens, wide, deep, seqs):
    chips = wide * deep
    plans = len(pairs)
    blocks, keys, width = own.shape
    articles = 2 * pairs[0][0].shape[0] // tokens
    shapes = [jax.ShapeDtypeStruct((articles, 128), jnp.float32)] * plans
    if others:
        rows = -(-(articles // seqs) // 8) * 8 * 2 * chips * seqs
        shapes.append(jax.ShapeDtypeStruct((rows, 128), jnp.float32))
    lines = -(-(plan_rows(chips, articles)[0] + 1) // 8) * 8
    work = plans * articles * 8
    smem, vmem = pl.BlockSpec(memory_space=pltpu.SMEM), pl.BlockSpec(memory_space=pltpu.VMEM)
    return pl.pallas_call(
        functools.partial(score_kernel, (plans, len(far), len(others), seqs, blocks, wide, deep)),
        out_shape=shapes,
        in_specs=[smem] + [vmem] * (2 * plans + len(far) + len(others) + 2),
        out_specs=[vmem] * len(shapes),
        scratch_shapes=[
            pltpu.VMEM((plans * articles, width, tokens), jnp.bfloat16),
            pltpu.VMEM((plans * articles, 8, tokens), jnp.float32),
            pltpu.VMEM((plans * (articles * NC + 8), tokens), jnp.float32),
            pltpu.VMEM((plans, lines, 128), jnp.int32),
            pltpu.SMEM((plans, lines, 128), jnp.int32),
            pltpu.SemaphoreType.DMA((plans,)),
        ],
        compiler_params=pltpu.CompilerParams(vmem_limit_bytes=32 * 1024 * 1024),
        cost_estimate=pl.CostEstimate(
            flops=int(SCOST * work * tokens * keys * width),
            bytes_accessed=4 * own.size,
            transcendentals=int(SCOST / 2 * work * tokens * keys),
        ),
        name="score_chunks",
    )(me, *[x for pair in pairs for x in pair], *far, *others, own, other)


def close_kernel(seqs, parts_ref, relevance_ref, probs_ref, score_ref):
    peers = parts_ref.shape[0]
    rows = relevance_ref.shape[0] // seqs
    for d in range(seqs):
        part = parts_ref[d]
        for j in range(d + seqs, peers, seqs):
            part = part + parts_ref[j]
        for i in range(rows):
            score_ref[i * seqs + d : i * seqs + d + 1, :] = part[i : i + 1]
    score = score_ref[:, 0:NC]
    relevance = score - jnp.mean(score, axis=-1, keepdims=True)
    weights = jnp.exp(TEMPER * relevance)
    relevance_ref[...] = relevance
    probs_ref[...] = weights / jnp.sum(weights, axis=-1, keepdims=True)


def close(parts, articles, seqs):
    vmem = pl.BlockSpec(memory_space=pltpu.VMEM)
    return pl.pallas_call(
        functools.partial(close_kernel, seqs),
        out_shape=[jax.ShapeDtypeStruct((articles, NC), jnp.float32)] * 2,
        in_specs=[vmem],
        out_specs=[vmem] * 2,
        scratch_shapes=[pltpu.VMEM((articles, 128), jnp.float32)],
        name="close",
    )(parts)


def per_device(wide, deep, queries, cand_owner, cand_local, companies):
    articles = queries.shape[0]
    seqs, arts = lax.axis_size("seq"), lax.axis_size("art")
    art, seq = lax.axis_index("art"), lax.axis_index("seq")
    chips = wide * deep
    half = chips // 2
    per_home = articles // seqs
    blocks = companies.shape[0]
    tokens = queries.shape[2]
    mine = queries.reshape(articles * tokens, queries.shape[3])
    ring = []
    for y in range(wide):
        for z in range(deep) if y % 2 == 0 else reversed(range(deep)):
            ring.append(z * wide + y)

    def turn(step, across=0):
        return [
            (
                (2 * ring[i] + c) * seqs + s,
                (2 * ring[(i + step) % chips] + c) * seqs + (s + across) % seqs,
            )
            for i in range(chips)
            for c in range(2)
            for s in range(seqs)
        ]

    def send(array, step, across=0):
        return lax.ppermute(array, ("art", "seq"), turn(step, across))

    cut = articles // 2 * tokens
    one, rest = mine[:cut], mine[cut:]
    ahead, behind = [None], [None]
    first = [send(one, 1), send(rest, -1)]

    ids = (cand_owner * blocks + cand_local).reshape(per_home, seqs * NC)
    ids = [ids] + [send(ids, 0, d) for d in range(1, seqs)]
    me = jnp.stack([art // 2, art % 2, seq]).astype(jnp.int32)
    two, back, lists = pack_streams(me, ids, one, rest, chips, blocks)
    second = [send(two, 1), send(back, -1)]
    ahead.append([first[0], second[0]])
    behind.append([first[1], second[1]])
    own = unit_blocks(lax.optimization_barrier((companies, *first))[0])
    other = lax.ppermute(companies, "art", [(i, i ^ 1) for i in range(arts)])
    other = unit_blocks(lax.optimization_barrier((other, *first))[0])

    def score(*pairs, far=(), others=()):
        return score_chunks(me, pairs, far, others, own, other, tokens, wide, deep, seqs)

    def after(array, *things):
        return lax.optimization_barrier((array, *things))[0]

    early = list(score((after(one, *second), two)))
    done = early[0]
    far = send(after(lists, done), half)
    for d in range(1, half):
        a, b = [ahead[d][0], behind[d][0]], [ahead[d][1], behind[d][1]]
        if d == 1:
            b = [after(x, own) for x in b]
        else:
            fresh = after(ahead[d - 1][0], done, *a, *([far] if d == 3 else []))
            more = score((fresh, ahead[d - 1][1]), behind[d - 1])
            early += more
            a = [after(x, done if d + 1 < half else more[0]) for x in a]
            b = [after(x, more[0]) for x in b]
            done = more[0]
        a, b = lax.optimization_barrier(a), lax.optimization_barrier(b)
        if d + 1 < half:
            ahead.append([send(a[0], 1), send(b[0], 1)])
            behind.append([send(a[1], -1), send(b[1], -1)])
        else:
            ahead[d][0] = a[0]
            last = (send(a[0], 1), send(a[1], -1))
    early += score(ahead[half - 1], behind[half - 1])
    spread = score(last, far=(far,), others=early)[1]
    parts = lax.all_to_all(spread, ("art", "seq"), split_axis=0, concat_axis=0, tiled=True)
    return tuple(close(parts.reshape(arts * seqs, -1, 128), articles, seqs))


def solution(mesh):
    chips = mesh.shape["art"] // 2
    wide = math.gcd(mesh.shape["seq"], chips)
    placed = (
        P("art", "seq", None, None),
        P(("art", "seq"), None, None),
        P(("art", "seq"), None, None),
        P("art", None, None),
    )
    return jax.shard_map(
        functools.partial(per_device, wide, chips // wide),
        mesh=mesh,
        in_specs=placed,
        out_specs=(P(("art", "seq"), None), P(("art", "seq"), None)),
        check_vma=False,
    )
```
